512 devices in a mesh: blk: 64 (over y_lo, z, core), rows: 8 (over x, y_hi).
Axes of the slice: x: 4, y: 8 (y_hi: 2, y_lo: 4; y = y_hi * 4 + y_lo), z: 8, core: 2. Of those that a mesh axis runs over, the one named last changes fastest.
Arguments:
- points: float32 [32, 131072], P(None, ('blk', 'rows')), may hold values from -6 to 6
- lengthscale: float32 [32], replicated, may hold values from 4 to 12
- noise_var: float32 [131072], P(('blk', 'rows')), may hold values from 0.5 to 2
- targets: float32 [64, 131072], P(None, ('blk', 'rows')), may hold values from -6 to 6
Outputs:
- solution: float32 [64, 131072], P(None, ('blk', 'rows'))
- residual: float32 [64, 131072], P(None, ('blk', 'rows'))
The draws below stay inside these ranges and needn't reach their ends.
All inputs are finite; a program needn't handle non-finite values.
Results may differ from the reference program's by a relative error of at most 0.011.
Values may be sent and summed in bfloat16 or wider, within the bound.
No kernel may reach another device: no remote copies, remote signals or barrier semaphores. Data moves between devices by JAX's collectives and lax.ppermute only.
A program may use at most 64 MiB of HBM per device.

```python
import math
import jax
import jax.numpy as jnp
from jax import lax

FEAT = 32
RHS = 64
BAND = 4
ITERS = 2
BLOCK = 2048
POINTS = 131072
N_BLK = 64


def block_scale(own_key, dims, split, low, largest):
    level, own = 1.0, jax.random.fold_in(own_key, 6)
    for dim, parts in split:
        heights = jnp.exp(jax.random.uniform(jax.random.fold_in(own, dim), (parts,), jnp.float32, low / len(split), largest / len(split)))
        level = level * jnp.repeat(heights, dims[dim] // parts).reshape([-1 if axis == dim else 1 for axis in range(len(dims))])
    return level


def gaussian(key, dims, spread, most, cuts=(), dtype=jnp.bfloat16):
    drawn = jax.random.normal(key, dims, jnp.float32) * spread
    if len(cuts) > 0:
        drawn = block_scale(key, dims, cuts, -0.22, 0.18) * drawn
    return jnp.clip(drawn, min=-most, max=most).astype(dtype)


def setup_inputs(seed: int = 0) -> dict:
    seeds = jax.random.split(jax.random.key(seed), 5)
    return {
        "points": gaussian(seeds[0], (FEAT, POINTS), 1.0, 6.0, ((1, 512),), jnp.float32),
        "lengthscale": jnp.clip(jnp.exp(jax.random.uniform(seeds[1], (FEAT,), jnp.float32, math.log(4.0), math.log(12.0))), 4.0, 12.0),
        "noise_var": jnp.clip(jnp.exp(math.log(2.0) - 1.3862944 * jax.random.uniform(seeds[2], (POINTS,), jnp.float32) ** block_scale(seeds[2], (POINTS,), ((0, 512),), -0.2, 0.2)), 0.5, 2.0),
        "targets": gaussian(seeds[3], (RHS, POINTS), 1.0, 6.0, ((1, 512),), jnp.float32),
    }


ROOT_FIVE = math.sqrt(5.0)

def matern_block(row_points, row_squares, col_points, col_squares, tapering):
    inner_prod = lax.dot_general(row_points, col_points, (((0,), (0,)), ((), ())), precision=lax.Precision.HIGHEST, preferred_element_type=jnp.float32)
    dist_sq = row_squares[:, None] + col_squares[None, :] - 2.0 * inner_prod
    scaled = ROOT_FIVE * jnp.sqrt(jnp.maximum(dist_sq, 0.0))
    values = (1.0 + scaled + scaled * scaled / 3.0) * jnp.exp(-scaled) * tapering
    return values.astype(jnp.bfloat16)

def forward(vectors, kernel_tile):
    return lax.dot_general(vectors, kernel_tile, (((1,), (1,)), ((), ())), preferred_element_type=jnp.float32)

def apply_kernel(direction, scaled, squares, noise_var):
    rounded = direction.astype(jnp.bfloat16)
    vec_blocks = rounded.reshape(RHS, N_BLK, BLOCK).transpose(1, 0, 2)
    pts_blocks = scaled.reshape(FEAT, N_BLK, BLOCK).transpose(1, 0, 2)
    sq_blocks = squares.reshape(N_BLK, BLOCK)
    summed = (noise_var[None, :] * direction).reshape(RHS, N_BLK, BLOCK).transpose(1, 0, 2)
    for distance in range(BAND):
        tapering = (BAND - distance) / BAND
        far_points = jnp.roll(pts_blocks, -distance, axis=0)
        far_squares = jnp.roll(sq_blocks, -distance, axis=0)
        far_vectors = jnp.roll(vec_blocks, -distance, axis=0)
        if distance == 0:

            def one_block(inputs):
                near_points, near_squares, col_points, col_squares, col_vectors = inputs
                return forward(col_vectors, matern_block(near_points, near_squares, col_points, col_squares, tapering))
            summed = summed + lax.map(one_block, (pts_blocks, sq_blocks, far_points, far_squares, far_vectors))
        else:

            def both_ways(inputs):
                near_points, near_squares, near_vectors, col_points, col_squares, col_vectors = inputs
                kernel_tile = matern_block(near_points, near_squares, col_points, col_squares, tapering)
                return (forward(col_vectors, kernel_tile), jnp.dot(near_vectors, kernel_tile, preferred_element_type=jnp.float32))
            ahead_part, behind = lax.map(both_ways, (pts_blocks, sq_blocks, vec_blocks, far_points, far_squares, far_vectors))
            summed = summed + ahead_part + jnp.roll(behind, distance, axis=0)
    return summed.transpose(1, 0, 2).reshape(RHS, POINTS)

def reference(points, lengthscale, noise_var, targets):
    scaled = points / lengthscale[:, None]
    squares = lax.optimization_barrier(jnp.sum(scaled * scaled, axis=0))
    solution = jnp.zeros_like(targets)
    residual = targets
    direction = targets
    norm_now = lax.optimization_barrier(jnp.sum(residual * residual, axis=1))
    for iteration in range(ITERS):
        applied = apply_kernel(direction, scaled, squares, noise_var)
        curvature = lax.optimization_barrier(jnp.sum(direction * applied, axis=1))
        step_size = norm_now / curvature
        solution = solution + step_size[:, None] * direction
        residual = residual - step_size[:, None] * applied
        norm_next = lax.optimization_barrier(jnp.sum(residual * residual, axis=1))
        direction = residual + (norm_next / norm_now)[:, None] * direction
        norm_now = norm_next
    return (solution, residual)
```

```python
import functools
import math

import jax
import jax.numpy as jnp
from jax import lax
from jax.experimental import pallas as pl
from jax.experimental.pallas import tpu as pltpu
from jax.sharding import Mesh, PartitionSpec as P

F32, BF16 = jnp.float32, jnp.bfloat16
AXES = ("y_lo", "z", "core", "x", "y_hi")
SIZES = (4, 8, 2, 4, 2)
BLK = ("y_lo", "z", "core")
N_BLK = 64
SWAP = ((0, 1), (1, 0))

LN2 = math.log(2.0)
UNIT = math.sqrt(5.0) / LN2
SHIFT = 1.5 / LN2
OFFSET = 0.75 / LN2**2
LEVEL = math.log2(LN2**2 / 3.0) + SHIFT
TINY = 1e-20

FEAT = 32
RHS = 64
WIDTH = 256
ROWS = 512
DEPTH = 144
NT = (((1,), (1,)), ((), ()))


def split(value):
    high = value.astype(BF16)
    return high, (value - high.astype(F32)).astype(BF16)


def square_rows(coords, first, second):
    squares = jnp.sum(coords * coords, axis=0, keepdims=True)
    one = squares.astype(BF16).astype(F32)
    two = (squares - one).astype(BF16).astype(F32)
    three = squares - one - two
    row = lax.broadcasted_iota(jnp.int32, (16, coords.shape[1]), 0)
    out = jnp.where((row >= second) & (row < second + 3), 1.0, 0.0)
    for at, piece in enumerate((one, two, three)):
        out = jnp.where(row == first + at, piece, out)
    return out.astype(BF16)


def build_shard(weights_ref, level, shard, cols_ref, dist_ref, kernel_ref):
    coords = shard[: 2 * FEAT]
    wide = coords.astype(F32)
    cols_ref[: 2 * FEAT] = coords
    cols_ref[2 * FEAT : 4 * FEAT] = coords
    cols_ref[4 * FEAT :] = square_rows(wide[:FEAT] + wide[FEAT:], 0, 3)
    dist_ref[...] = jnp.dot(weights_ref[...], cols_ref[...], preferred_element_type=F32)
    step = 64
    for at in range(0, ROWS, step):
        part = jnp.maximum(dist_ref[at : at + step], TINY)
        moved = part * lax.rsqrt(part) + SHIFT
        entry = (moved * moved + OFFSET) * jnp.exp2(level - moved)
        kernel_ref[at : at + step] = entry.astype(BF16)
    return lax.dot_general(shard[2 * FEAT :], kernel_ref[...], NT, preferred_element_type=F32)


def build_first(levels, own_ref, peer_ref, block_ref, weights_ref, total_ref, kernel_ref, cols_ref, dist_ref):
    for at, ref in enumerate((own_ref, peer_ref)):
        coords = ref[: 2 * FEAT].astype(F32)
        high, low = coords[:FEAT], coords[FEAT:]
        extra = square_rows(high + low, 3, 0).astype(F32)
        stacked = jnp.concatenate([-2.0 * high, -2.0 * high, -2.0 * low, -2.0 * low], axis=0)
        weights_ref[at * WIDTH : (at + 1) * WIDTH, : 4 * FEAT] = jnp.transpose(stacked).astype(BF16)
        weights_ref[at * WIDTH : (at + 1) * WIDTH, 4 * FEAT :] = jnp.transpose(extra).astype(BF16)
    total_ref[...] = jnp.zeros_like(total_ref)

    def one(i, carry):
        total_ref[...] += build_shard(weights_ref, levels[0], block_ref[i], cols_ref, dist_ref, kernel_ref.at[i])
        return carry

    lax.fori_loop(0, block_ref.shape[0], one, 0)


def build_more(level_ref, weights_ref, before_ref, *refs):
    count = level_ref.shape[0]
    blocks, (total_ref, kernel_ref, cols_ref, dist_ref) = refs[:count], refs[count:]
    total_ref[...] = before_ref[...]
    for at, block_ref in enumerate(blocks):
        level = level_ref[at]

        def one(i, carry, at=at, block_ref=block_ref, level=level):
            total_ref[...] += build_shard(
                weights_ref, level, block_ref[i], cols_ref, dist_ref, kernel_ref.at[at * 4 + i]
            )
            return carry

        lax.fori_loop(0, block_ref.shape[0], one, 0)


def add_blocks(total_ref, kernel_ref, blocks):
    for at, block_ref in enumerate(blocks):

        def one(i, carry, at=at, block_ref=block_ref):
            both = lax.dot_general(block_ref[i], kernel_ref[at * 4 + i], NT, preferred_element_type=F32)
            total_ref[...] += both[:RHS] + both[RHS:]
            return carry

        lax.fori_loop(0, block_ref.shape[0], one, 0)


def apply_first(kernel_ref, *refs):
    total_ref = refs[-1]
    total_ref[...] = jnp.zeros_like(total_ref)
    add_blocks(total_ref, kernel_ref, refs[:-1])


def apply_more(kernel_ref, before_ref, *refs):
    total_ref = refs[-1]
    total_ref[...] = before_ref[...]
    add_blocks(total_ref, kernel_ref, refs[:-1])


def row_sums(product):
    ones = jnp.ones((8, product.shape[1]), F32)
    return lax.dot_general(ones, product, NT, precision=lax.Precision.HIGHEST, preferred_element_type=F32)


def apply_last(kernel_ref, before_ref, noise_ref, first_ref, peer_first_ref, image_ref, peer_image_ref, *refs):
    total_ref, sums_ref = refs[-2:]
    total_ref[...] = before_ref[...]
    add_blocks(total_ref, kernel_ref, refs[:-2])
    first, image = first_ref[...], image_ref[...]
    peer = peer_image_ref[...].astype(F32)
    peer_image = peer[:RHS] + peer[RHS:]
    peer = peer_first_ref[2 * FEAT :].astype(F32)
    peer_first = peer[:RHS] + peer[RHS:]
    near = total_ref[:, :WIDTH] + noise_ref[...] * image
    far = total_ref[:, WIDTH:]
    rows = (
        first * first,
        first * image,
        image * image,
        first * near + peer_first * far,
        image * near + peer_image * far,
    )
    at = lax.broadcasted_iota(jnp.int32, (8, RHS), 0)
    out = jnp.zeros((8, RHS), F32)
    for i, row in enumerate(rows):
        out = jnp.where(at == i, row_sums(row), out)
    sums_ref[:, :RHS] = out
    sums_ref[:, RHS:] = jnp.zeros_like(out)


VMEM_LIMIT = pltpu.CompilerParams(vmem_limit_bytes=48 * 1024 * 1024)
SMEM = pl.BlockSpec(memory_space=pltpu.SMEM)
VMEM = pl.BlockSpec(memory_space=pltpu.VMEM)


def scratch():
    return [pltpu.VMEM((DEPTH, WIDTH), BF16), pltpu.VMEM((ROWS, WIDTH), F32)]


def shape(*dims, dtype=F32):
    return jax.ShapeDtypeStruct(dims, dtype)


def shifted(value, distance):
    route = [((i - distance) % N_BLK, i) for i in range(N_BLK)]
    return lax.ppermute(value, BLK, route)


def gathered(value, axes):
    count = math.prod(SIZES[AXES.index(axis)] for axis in axes)
    return lax.all_to_all(jnp.broadcast_to(value[None], (count,) + value.shape), axes, 0, 0)


def halo(block):
    swapped = lax.ppermute(block, "core", SWAP)
    up, down = shifted(block, 2), shifted(block, -2)
    third = [(i, (i - 3 if i % 2 == 0 else i + 3) % N_BLK) for i in range(N_BLK)]
    far = lax.ppermute(block, BLK, third)
    up_swapped = lax.ppermute(up, "core", SWAP)
    down_swapped = lax.ppermute(down, "core", SWAP)
    return swapped, far, up, down, up_swapped, down_swapped


def body(points, lengthscale, noise_var, targets):
    coords = points / lengthscale[:, None] * UNIT
    message = jnp.concatenate(split(coords) + split(targets), axis=0)
    block = gathered(message[: 2 * FEAT + RHS], ("x",))
    peer_message = lax.ppermute(message, "y_hi", SWAP)
    swapped, far, up, down, up_swapped, down_swapped = halo(block)

    levels = [LEVEL + math.log2(taper) for taper in (1.0, 0.75, 0.5, 0.25)]
    odd = lax.axis_index("core") == 1
    edge = (jnp.where(odd, levels[3], levels[1]), jnp.where(odd, levels[1], levels[3]))
    weights, total, kernel_own = pl.pallas_call(
        functools.partial(build_first, levels),
        out_shape=(shape(ROWS, DEPTH, dtype=BF16), shape(RHS, ROWS), shape(4, ROWS, WIDTH, dtype=BF16)),
        scratch_shapes=scratch(),
        compiler_params=VMEM_LIMIT,
    )(message, peer_message, block)
    kernels = []
    for pair, pair_levels in (
        ((swapped, far), (levels[1], levels[3])),
        ((up, down), (levels[2], levels[2])),
        ((up_swapped, down_swapped), edge),
    ):
        total, made = pl.pallas_call(
            build_more,
            in_specs=[SMEM] + [VMEM] * 4,
            out_shape=(shape(RHS, ROWS), shape(8, ROWS, WIDTH, dtype=BF16)),
            scratch_shapes=scratch(),
            compiler_params=VMEM_LIMIT,
        )(jnp.stack([jnp.asarray(level, F32) for level in pair_levels]), weights, total, *pair)
        kernels.append(made)

    noise = noise_var[None, :]
    image = noise * targets + total[:, :WIDTH] + lax.ppermute(total[:, WIDTH:], "y_hi", SWAP)
    image_message = jnp.concatenate(split(image), axis=0)
    block = gathered(image_message, ("x",))
    peer_image = lax.ppermute(image_message, "y_hi", SWAP)
    swapped, far, up, down, up_swapped, down_swapped = halo(block)
    total = pl.pallas_call(apply_first, out_shape=shape(RHS, ROWS), compiler_params=VMEM_LIMIT)(kernel_own, block)
    for made, pair in zip(kernels[:2], ((swapped, far), (up, down))):
        total = pl.pallas_call(apply_more, out_shape=shape(RHS, ROWS), compiler_params=VMEM_LIMIT)(made, total, *pair)
    total, sums = pl.pallas_call(
        apply_last,
        out_shape=(shape(RHS, ROWS), shape(8, 2 * RHS)),
        compiler_params=VMEM_LIMIT,
    )(kernels[2], total, noise, targets, peer_message, image, peer_image, up_swapped, down_swapped)
    second = noise * image + total[:, :WIDTH] + lax.ppermute(total[:, WIDTH:], "y_hi", SWAP)
    for axes in (("x", "y_hi", "y_lo"), ("z", "core")):
        sums = jnp.sum(gathered(sums, axes), axis=0)

    rr, rq, qq, rs, qs = (sums[i, :RHS] for i in range(5))
    step = rr / rq
    norm_next = jnp.maximum(rr - 2.0 * step * rq + step * step * qq, 0.0)
    grown = 1.0 + norm_next / rr
    curvature = grown * grown * rq - step * grown * (qq + rs) + step * step * qs
    step_next = norm_next / curvature
    along = (step + step_next * grown)[:, None]
    across = (step_next * step)[:, None]
    solution = along * targets - across * image
    residual = targets - along * image + across * second
    return solution, residual


def solution(mesh):
    fine = Mesh(mesh.devices.reshape(SIZES), AXES)
    placed = (P(None, AXES), P(), P(AXES), P(None, AXES))
    return jax.shard_map(
        body, mesh=fine, in_specs=placed, out_specs=(P(None, AXES), P(None, AXES)), check_vma=False
    )
```

```python
import math

import jax
import jax.numpy as jnp
from jax import lax
from jax.experimental import pallas as pl
from jax.experimental.pallas import tpu as pltpu
from jax.sharding import Mesh, PartitionSpec as P

F32, BF16 = jnp.float32, jnp.bfloat16
AXES = ("y_lo", "z", "core", "x", "y_hi")
SIZES = (4, 8, 2, 4, 2)
BLK = ("y_lo", "z", "core")
N_BLK = 64
SWAP = ((0, 1), (1, 0))

LN2 = math.log(2.0)
UNIT = math.sqrt(5.0) / LN2
SHIFT = 1.5 / LN2
OFFSET = 0.75 / LN2**2
LEVEL = math.log2(LN2**2 / 3.0) + SHIFT
TINY = 1e-20

FEAT = 32
RHS = 64
WIDTH = 256
DEPTH = 144
SHARDS = 8
SIGMA = 0.5
NT = (((1,), (1,)), ((), ()))


def split(value):
    high = lax.reduce_precision(value, 8, 7)
    return high.astype(BF16), (value - high).astype(BF16)


def square_rows(coords, first, second):
    squares = jnp.sum(coords * coords, axis=0, keepdims=True)
    one = squares.astype(BF16).astype(F32)
    two = (squares - one).astype(BF16).astype(F32)
    three = squares - one - two
    row = lax.broadcasted_iota(jnp.int32, (16, coords.shape[1]), 0)
    out = jnp.where((row >= second) & (row < second + 3), 1.0, 0.0)
    for at, piece in enumerate((one, two, three)):
        out = jnp.where(row == first + at, piece, out)
    return out.astype(BF16)


def build_shard(weights, level, shard, cols_ref, dist_ref, kernel_ref):
    coords = shard[: 2 * FEAT]
    wide = coords.astype(F32)
    cols_ref[: 2 * FEAT] = coords
    cols_ref[2 * FEAT : 4 * FEAT] = coords
    cols_ref[4 * FEAT :] = square_rows(wide[:FEAT] + wide[FEAT:], 0, 3)
    dist_ref[...] = jnp.dot(weights, cols_ref[...], preferred_element_type=F32)
    step = 64
    for at in range(0, WIDTH, step):
        part = jnp.maximum(dist_ref[at : at + step], TINY)
        moved = part * lax.rsqrt(part) + SHIFT
        entry = (moved * moved + OFFSET) * jnp.exp2(level - moved)
        kernel_ref[at : at + step] = entry.astype(BF16)
    return lax.dot_general(shard[2 * FEAT :], kernel_ref[...], NT, preferred_element_type=F32)


def build_block(weights, level, block_ref, cols_ref, dist_ref, kernel_ref):
    total = None
    for i in range(SHARDS):
        part = build_shard(weights, level, block_ref[i], cols_ref.at[i % 2], dist_ref.at[i % 2], kernel_ref.at[i])
        total = part if total is None else total + part
    return total


def build_first(own_ref, block_ref, weights_ref, total_ref, kernel_ref, cols_ref, dist_ref):
    coords = own_ref[: 2 * FEAT].astype(F32)
    high, low = coords[:FEAT], coords[FEAT:]
    extra = square_rows(high + low, 3, 0).astype(F32)
    stacked = jnp.concatenate([-2.0 * high, -2.0 * high, -2.0 * low, -2.0 * low], axis=0)
    weights_ref[:, : 4 * FEAT] = jnp.transpose(stacked).astype(BF16)
    weights_ref[:, 4 * FEAT :] = jnp.transpose(extra).astype(BF16)
    total_ref[...] = build_block(weights_ref[...], LEVEL, block_ref, cols_ref, dist_ref, kernel_ref.at[0])


def build_more(level_ref, weights_ref, before_ref, *refs):
    count = level_ref.shape[0]
    blocks, (total_ref, kernel_ref, cols_ref, dist_ref) = refs[:count], refs[count:]
    total = before_ref[...]
    for at, block_ref in enumerate(blocks):
        total = total + build_block(
            weights_ref[...], level_ref[at], block_ref, cols_ref, dist_ref, kernel_ref.at[at]
        )
    total_ref[...] = total


def add_blocks(total, kernel_ref, blocks):
    for at, block_ref in enumerate(blocks):
        for i in range(SHARDS):
            total = total + lax.dot_general(block_ref[i], kernel_ref[at, i], NT, preferred_element_type=F32)
    return total


def apply_first(kernel_ref, *refs):
    refs[-1][...] = add_blocks(jnp.zeros((RHS, WIDTH), F32), kernel_ref, refs[:-1])


def apply_more(kernel_ref, before_ref, *refs):
    refs[-1][...] = add_blocks(before_ref[...], kernel_ref, refs[:-1])


def row_sums(product):
    ones = jnp.ones((8, product.shape[1]), F32)
    return lax.dot_general(ones, product, NT, precision=lax.Precision.HIGHEST, preferred_element_type=F32)


def apply_last(kernel_ref, before_ref, noise_ref, first_ref, first_total_ref, image_ref, *refs):
    second_ref, sums_ref = refs[-2:]
    total = add_blocks(before_ref[...], kernel_ref, refs[:-2])
    first, image = first_ref[...], image_ref[...]
    second = noise_ref[...] * image + (first_total_ref[...] - total) * (1.0 / SIGMA)
    second_ref[...] = second
    rows = (first * first, first * image, image * image, first * second, image * second)
    at = lax.broadcasted_iota(jnp.int32, (8, RHS), 0)
    out = jnp.zeros((8, RHS), F32)
    for i, row in enumerate(rows):
        out = jnp.where(at == i, row_sums(row), out)
    sums_ref[:, :RHS] = out
    sums_ref[:, RHS:] = jnp.zeros_like(out)


VMEM_LIMIT = pltpu.CompilerParams(vmem_limit_bytes=48 * 1024 * 1024)
SMEM = pl.BlockSpec(memory_space=pltpu.SMEM)
VMEM = pl.BlockSpec(memory_space=pltpu.VMEM)


def scratch():
    return [pltpu.VMEM((2, DEPTH, WIDTH), BF16), pltpu.VMEM((2, WIDTH, WIDTH), F32)]


def shape(*dims, dtype=F32):
    return jax.ShapeDtypeStruct(dims, dtype)


def shifted(value, distance):
    route = [((i - distance) % N_BLK, i) for i in range(N_BLK)]
    return lax.ppermute(value, BLK, route)


def gathered(value, axes):
    count = math.prod(SIZES[AXES.index(axis)] for axis in axes)
    return lax.all_to_all(jnp.broadcast_to(value[None], (count,) + value.shape), axes, 0, 0)


def halo(block):
    swapped = lax.ppermute(block, "core", SWAP)
    up, down = shifted(block, 2), shifted(block, -2)
    third = [(i, (i - 3 if i % 2 == 0 else i + 3) % N_BLK) for i in range(N_BLK)]
    far = lax.ppermute(block, BLK, third)
    up_swapped = lax.ppermute(up, "core", SWAP)
    down_swapped = lax.ppermute(down, "core", SWAP)
    return swapped, far, up, down, up_swapped, down_swapped


def kernel_shape(blocks):
    return shape(blocks, SHARDS, WIDTH, WIDTH, dtype=BF16)


def body(points, lengthscale, noise_var, targets):
    coords = points / lengthscale[:, None] * UNIT
    message = jnp.concatenate(split(coords) + (targets.astype(BF16),), axis=0)
    block = gathered(message, ("x", "y_hi"))
    swapped, far, up, down, up_swapped, down_swapped = halo(block)

    levels = [LEVEL + math.log2(taper) for taper in (1.0, 0.75, 0.5, 0.25)]
    odd = lax.axis_index("core") == 1
    edge = (jnp.where(odd, levels[3], levels[1]), jnp.where(odd, levels[1], levels[3]))
    weights, total, made = pl.pallas_call(
        build_first,
        out_shape=(shape(WIDTH, DEPTH, dtype=BF16), shape(RHS, WIDTH), kernel_shape(1)),
        scratch_shapes=scratch(),
        compiler_params=VMEM_LIMIT,
    )(message, block)
    kernels = [made]
    for blocks, block_levels in (
        ((swapped,), (levels[1],)),
        ((far,), (levels[3],)),
        ((up, down), (levels[2], levels[2])),
        ((up_swapped, down_swapped), edge),
    ):
        total, made = pl.pallas_call(
            build_more,
            in_specs=[SMEM] + [VMEM] * (2 + len(blocks)),
            out_shape=(shape(RHS, WIDTH), kernel_shape(len(blocks))),
            scratch_shapes=scratch(),
            compiler_params=VMEM_LIMIT,
        )(jnp.stack([jnp.asarray(level, F32) for level in block_levels]), weights, total, *blocks)
        kernels.append(made)

    noise = noise_var[None, :]
    image = noise * targets + total
    block = gathered((targets - SIGMA * image).astype(BF16), ("x", "y_hi"))
    swapped, far, up, down, up_swapped, down_swapped = halo(block)
    sent = pl.pallas_call(apply_first, out_shape=shape(RHS, WIDTH), compiler_params=VMEM_LIMIT)(kernels[0], block)
    for made, blocks in zip(kernels[1:4], ((swapped,), (far,), (up, down))):
        sent = pl.pallas_call(apply_more, out_shape=shape(RHS, WIDTH), compiler_params=VMEM_LIMIT)(made, sent, *blocks)
    second, sums = pl.pallas_call(
        apply_last, out_shape=(shape(RHS, WIDTH), shape(8, 2 * RHS)), compiler_params=VMEM_LIMIT
    )(kernels[4], sent, noise, targets, total, image, up_swapped, down_swapped)
    for axes in (("x", "y_hi", "y_lo"), ("z", "core")):
        sums = jnp.sum(gathered(sums, axes), axis=0)

    rr, rq, qq, rs, qs = (sums[i, :RHS] for i in range(5))
    step = rr / rq
    norm_next = jnp.maximum(rr - 2.0 * step * rq + step * step * qq, 0.0)
    grown = 1.0 + norm_next / rr
    curvature = grown * grown * rq - step * grown * (qq + rs) + step * step * qs
    step_next = norm_next / curvature
    along = (step + step_next * grown)[:, None]
    across = (step_next * step)[:, None]
    solution = along * targets - across * image
    residual = targets - along * image + across * second
    return solution, residual


def solution(mesh):
    fine = Mesh(mesh.devices.reshape(SIZES), AXES)
    placed = (P(None, AXES), P(), P(AXES), P(None, AXES))
    return jax.shard_map(
        body, mesh=fine, in_specs=placed, out_specs=(P(None, AXES), P(None, AXES)), check_vma=False
    )
```

```python
import math

import jax
import jax.numpy as jnp
from jax import lax
from jax.experimental import pallas as pl
from jax.experimental.pallas import tpu as pltpu
from jax.sharding import Mesh, PartitionSpec as P

F32, BF16 = jnp.float32, jnp.bfloat16
AXES = ("y_lo", "z", "core", "x", "y_hi")
SIZES = (4, 8, 2, 4, 2)
BLK = ("y_lo", "z", "core")
N_BLK = 64
SWAP = ((0, 1), (1, 0))

LN2 = math.log(2.0)
UNIT = math.sqrt(5.0) / LN2
SHIFT = 1.5 / LN2
OFFSET = 0.75 / LN2**2
LEVEL = math.log2(LN2**2 / 3.0) + SHIFT
LEVELS = tuple(LEVEL + math.log2(taper) for taper in (1.0, 0.75, 0.5, 0.25))
TINY = 1e-20

FEAT = 32
RHS = 64
WIDTH = 256
DEPTH = 144
SHARDS = 8
SIGMA = 0.5
NT = (((1,), (1,)), ((), ()))


def split(value):
    high = lax.reduce_precision(value, 8, 7)
    return high.astype(BF16), (value - high).astype(BF16)


def square_rows(coords, first, second):
    squares = jnp.sum(coords * coords, axis=0, keepdims=True)
    one = squares.astype(BF16).astype(F32)
    two = (squares - one).astype(BF16).astype(F32)
    three = squares - one - two
    row = lax.broadcasted_iota(jnp.int32, (16, coords.shape[1]), 0)
    out = jnp.where((row >= second) & (row < second + 3), 1.0, 0.0)
    for at, piece in enumerate((one, two, three)):
        out = jnp.where(row == first + at, piece, out)
    return out.astype(BF16)


def build_shard(weights, levels, shard, cols_ref, dist_ref, kernel_ref):
    coords = shard[: 2 * FEAT]
    wide = coords.astype(F32)
    cols_ref[: 2 * FEAT] = coords
    cols_ref[2 * FEAT : 4 * FEAT] = coords
    cols_ref[4 * FEAT :] = square_rows(wide[:FEAT] + wide[FEAT:], 0, 3)
    dist_ref[...] = jnp.dot(weights, cols_ref[...], preferred_element_type=F32)
    step = 64
    for half, level in enumerate(levels):
        for at in range(half * WIDTH, (half + 1) * WIDTH, step):
            part = jnp.maximum(dist_ref[at : at + step], TINY)
            moved = part * lax.rsqrt(part) + SHIFT
            entry = (moved * moved + OFFSET) * jnp.exp2(level - moved)
            kernel_ref[at : at + step] = entry.astype(BF16)
    return lax.dot_general(shard[2 * FEAT :], kernel_ref[...], NT, preferred_element_type=F32)


def build_block(weights, levels, block_ref, cols_ref, dist_ref, kernel_ref):
    total = None
    for i in range(SHARDS):
        part = build_shard(weights, levels, block_ref[i], cols_ref.at[i % 2], dist_ref.at[i % 2], kernel_ref.at[i])
        total = part if total is None else total + part
    return total


def build_first(own_ref, peer_ref, block_ref, weights_ref, total_ref, kernel_ref, cols_ref, dist_ref):
    for at, ref in enumerate((own_ref, peer_ref)):
        rows = slice(at * WIDTH, (at + 1) * WIDTH)
        coords = ref[: 2 * FEAT].astype(F32)
        high, low = coords[:FEAT], coords[FEAT:]
        extra = square_rows(high + low, 3, 0).astype(F32)
        stacked = jnp.concatenate([-2.0 * high, -2.0 * high, -2.0 * low, -2.0 * low], axis=0)
        weights_ref[rows, : 4 * FEAT] = jnp.transpose(stacked).astype(BF16)
        weights_ref[rows, 4 * FEAT :] = jnp.transpose(extra).astype(BF16)
    total_ref[...] = build_block(weights_ref[...], LEVELS[:2], block_ref, cols_ref, dist_ref, kernel_ref)


def build_more(level_ref, weights_ref, before_ref, block_ref, total_ref, kernel_ref, cols_ref, dist_ref):
    levels = (level_ref[0], level_ref[1])
    total_ref[...] = before_ref[...] + build_block(
        weights_ref[...], levels, block_ref, cols_ref, dist_ref, kernel_ref
    )


def build_far(weights_ref, before_ref, block_ref, total_ref, kernel_ref, cols_ref, dist_ref):
    total_ref[...] = before_ref[:, WIDTH:] + build_block(
        weights_ref[WIDTH:], LEVELS[3:], block_ref, cols_ref, dist_ref, kernel_ref
    )


def add_block(total, kernel_ref, block_ref):
    for i in range(SHARDS):
        total = total + lax.dot_general(block_ref[i], kernel_ref[i], NT, preferred_element_type=F32)
    return total


def apply_first(kernel_ref, block_ref, total_ref):
    total_ref[...] = add_block(jnp.zeros(total_ref.shape, F32), kernel_ref, block_ref)


def apply_more(kernel_ref, before_ref, block_ref, total_ref):
    total_ref[...] = add_block(before_ref[...], kernel_ref, block_ref)


def apply_far(kernel_ref, before_ref, block_ref, total_ref):
    total_ref[...] = add_block(before_ref[:, WIDTH:], kernel_ref, block_ref)


def row_sums(sums_ref, at, products):
    ones = jnp.ones((8, WIDTH), F32)
    row = lax.broadcasted_iota(jnp.int32, (8, RHS), 0)
    out = jnp.zeros((8, RHS), F32)
    for i, product in enumerate(products):
        total = lax.dot_general(ones, product, NT, precision=lax.Precision.HIGHEST, preferred_element_type=F32)
        out = jnp.where(row == at + i, total, out)
    sums_ref[:, :RHS] = out
    sums_ref[:, RHS:] = jnp.zeros_like(out)


def early_sums(first_ref, image_ref, sums_ref):
    first, image = first_ref[...], image_ref[...]
    row_sums(sums_ref, 0, (first * first, first * image, image * image))


def late_sums(early_ref, noise_ref, first_ref, first_total_ref, image_ref, own_ref, peer_ref, second_ref, sums_ref):
    first, image = first_ref[...], image_ref[...]
    total = own_ref[:, :WIDTH] + peer_ref[...]
    second = noise_ref[...] * image + (first_total_ref[...] - total) * (1.0 / SIGMA)
    second_ref[...] = second
    row_sums(sums_ref, 3, (first * second, image * second))
    sums_ref[...] += early_ref[...]


VMEM_LIMIT = pltpu.CompilerParams(vmem_limit_bytes=48 * 1024 * 1024)
SMEM = pl.BlockSpec(memory_space=pltpu.SMEM)
VMEM = pl.BlockSpec(memory_space=pltpu.VMEM)


def scratch(rows=2 * WIDTH):
    return [pltpu.VMEM((2, DEPTH, WIDTH), BF16), pltpu.VMEM((2, rows, WIDTH), F32)]


def shape(*dims, dtype=F32):
    return jax.ShapeDtypeStruct(dims, dtype)


def shifted(value, distance):
    route = [((i - distance) % N_BLK, i) for i in range(N_BLK)]
    return lax.ppermute(value, BLK, route)


def gathered(value, axes):
    count = math.prod(SIZES[AXES.index(axis)] for axis in axes)
    return lax.all_to_all(jnp.broadcast_to(value[None], (count,) + value.shape), axes, 0, 0)


def halo(block):
    fourth = [(i, (i - 4 if i % 2 == 0 else i + 4) % N_BLK) for i in range(N_BLK)]
    return lax.ppermute(block, BLK, fourth), shifted(block, 2), shifted(block, -2)


def kernel_shape(rows=2 * WIDTH):
    return shape(SHARDS, rows, WIDTH, dtype=BF16)


def call(body, out_shape, in_specs=None, scratch_shapes=()):
    extra = {} if in_specs is None else {"in_specs": in_specs}
    return pl.pallas_call(
        body, out_shape=out_shape, scratch_shapes=scratch_shapes, compiler_params=VMEM_LIMIT, **extra
    )


def body(points, lengthscale, noise_var, targets):
    coords = points / lengthscale[:, None] * UNIT
    message = jnp.concatenate(split(coords) + (targets.astype(BF16),), axis=0)
    block = gathered(message, ("x", "y_hi"))
    peer = lax.ppermute(message[: 2 * FEAT], "core", SWAP)
    far, up, down = halo(block)

    odd = lax.axis_index("core") == 1
    near_far = jnp.where(odd, LEVELS[1], LEVELS[3]), jnp.where(odd, LEVELS[3], LEVELS[1])
    weights, total, kernel_own = call(
        build_first,
        (shape(2 * WIDTH, DEPTH, dtype=BF16), shape(RHS, 2 * WIDTH), kernel_shape()),
        scratch_shapes=scratch(),
    )(message, peer, block)
    kernels = []
    for moved, level in zip((up, down), near_far):
        total, made = call(
            build_more,
            (shape(RHS, 2 * WIDTH), kernel_shape()),
            in_specs=[SMEM] + [VMEM] * 3,
            scratch_shapes=scratch(),
        )(jnp.stack([jnp.asarray(LEVELS[2], F32), level]), weights, total, moved)
        kernels.append(made)
    peer_total, kernel_far = call(
        build_far, (shape(RHS, WIDTH), kernel_shape(WIDTH)), scratch_shapes=scratch(WIDTH)
    )(weights, total, far)

    noise = noise_var[None, :]
    first_total = total[:, :WIDTH] + lax.ppermute(peer_total, "core", SWAP)
    image = noise * targets + first_total
    block = gathered((targets - SIGMA * image).astype(BF16), ("x", "y_hi"))
    far, up, down = halo(block)
    early = call(early_sums, shape(8, 2 * RHS))(targets, image)
    total = call(apply_first, shape(RHS, 2 * WIDTH))(kernel_own, block)
    for made, moved in zip(kernels, (up, down)):
        total = call(apply_more, shape(RHS, 2 * WIDTH))(made, total, moved)
    peer_total = call(apply_far, shape(RHS, WIDTH))(kernel_far, total, far)
    peer_total = lax.ppermute(peer_total, "core", SWAP)
    second, sums = call(late_sums, (shape(RHS, WIDTH), shape(8, 2 * RHS)))(
        early, noise, targets, first_total, image, total, peer_total
    )
    for axes in (("x", "y_hi", "y_lo"), ("z", "core")):
        sums = jnp.sum(gathered(sums, axes), axis=0)

    rr, rq, qq, rs, qs = (sums[i, :RHS] for i in range(5))
    step = rr / rq
    norm_next = jnp.maximum(rr - 2.0 * step * rq + step * step * qq, 0.0)
    grown = 1.0 + norm_next / rr
    curvature = grown * grown * rq - step * grown * (qq + rs) + step * step * qs
    step_next = norm_next / curvature
    along = (step + step_next * grown)[:, None]
    across = (step_next * step)[:, None]
    solution = along * targets - across * image
    residual = targets - along * image + across * second
    return solution, residual


def solution(mesh):
    fine = Mesh(mesh.devices.reshape(SIZES), AXES)
    placed = (P(None, AXES), P(), P(AXES), P(None, AXES))
    return jax.shard_map(
        body, mesh=fine, in_specs=placed, out_specs=(P(None, AXES), P(None, AXES)), check_vma=False
    )
```

```python
import math

import jax
import jax.numpy as jnp
from jax import lax
from jax.experimental import pallas as pl
from jax.experimental.pallas import tpu as pltpu
from jax.sharding import Mesh, PartitionSpec as P

F32, BF16 = jnp.float32, jnp.bfloat16
AXES = ("y_lo", "z", "core", "x", "y_hi")
SIZES = (4, 8, 2, 4, 2)
BLK = ("y_lo", "z", "core")
N_BLK = 64
SWAP = ((0, 1), (1, 0))

LN2 = math.log(2.0)
UNIT = math.sqrt(5.0) / LN2
SHIFT = 1.5 / LN2
OFFSET = 0.75 / LN2**2
LEVEL = math.log2(LN2**2 / 3.0) + SHIFT
LEVELS = tuple(LEVEL + math.log2(taper) for taper in (1.0, 0.75, 0.5, 0.25))
TINY = 1e-20

FEAT = 32
RHS = 64
WIDTH = 256
DEPTH = 144
SHARDS = 8
SIGMA = 0.5
NT = (((1,), (1,)), ((), ()))


def split(value):
    high = lax.reduce_precision(value, 8, 7)
    return high.astype(BF16), (value - high).astype(BF16)


def square_rows(coords, first, second):
    squares = jnp.sum(coords * coords, axis=0, keepdims=True)
    one = squares.astype(BF16).astype(F32)
    two = (squares - one).astype(BF16).astype(F32)
    three = squares - one - two
    row = lax.broadcasted_iota(jnp.int32, (16, coords.shape[1]), 0)
    out = jnp.where((row >= second) & (row < second + 3), 1.0, 0.0)
    for at, piece in enumerate((one, two, three)):
        out = jnp.where(row == first + at, piece, out)
    return out.astype(BF16)


def build_shard(weights, levels, shard, cols_ref, dist_ref, kernel_ref):
    coords = shard[: 2 * FEAT]
    wide = coords.astype(F32)
    cols_ref[: 2 * FEAT] = coords
    cols_ref[2 * FEAT : 4 * FEAT] = coords
    cols_ref[4 * FEAT :] = square_rows(wide[:FEAT] + wide[FEAT:], 0, 3)
    dist_ref[...] = jnp.dot(weights, cols_ref[...], preferred_element_type=F32)
    step = 64
    for half, level in enumerate(levels):
        for at in range(half * WIDTH, (half + 1) * WIDTH, step):
            part = jnp.maximum(dist_ref[at : at + step], TINY)
            moved = part * lax.rsqrt(part) + SHIFT
            entry = (moved * moved + OFFSET) * jnp.exp2(level - moved)
            kernel_ref[at : at + step] = entry.astype(BF16)
    return lax.dot_general(shard[2 * FEAT :], kernel_ref[...], NT, preferred_element_type=F32)


def build_block(weights, levels, block_ref, cols_ref, dist_ref, kernel_ref):
    total = None
    for i in range(SHARDS):
        part = build_shard(weights, levels, block_ref[i], cols_ref.at[i % 2], dist_ref.at[i % 2], kernel_ref.at[i])
        total = part if total is None else total + part
    return total


def build_first(own_ref, peer_ref, block_ref, weights_ref, total_ref, kernel_ref, cols_ref, dist_ref):
    for at, ref in enumerate((own_ref, peer_ref)):
        rows = slice(at * WIDTH, (at + 1) * WIDTH)
        coords = ref[: 2 * FEAT].astype(F32)
        high, low = coords[:FEAT], coords[FEAT:]
        extra = square_rows(high + low, 3, 0).astype(F32)
        stacked = jnp.concatenate([-2.0 * high, -2.0 * high, -2.0 * low, -2.0 * low], axis=0)
        weights_ref[rows, : 4 * FEAT] = jnp.transpose(stacked).astype(BF16)
        weights_ref[rows, 4 * FEAT :] = jnp.transpose(extra).astype(BF16)
    total_ref[...] = build_block(weights_ref[...], LEVELS[:2], block_ref, cols_ref, dist_ref, kernel_ref)


def build_more(level_ref, weights_ref, before_ref, block_ref, total_ref, kernel_ref, cols_ref, dist_ref):
    levels = (level_ref[0], level_ref[1])
    total_ref[...] = before_ref[...] + build_block(
        weights_ref[...], levels, block_ref, cols_ref, dist_ref, kernel_ref
    )


def build_far(weights_ref, before_ref, block_ref, total_ref, kernel_ref, cols_ref, dist_ref):
    total_ref[...] = before_ref[:, WIDTH:] + build_block(
        weights_ref[WIDTH:], LEVELS[3:], block_ref, cols_ref, dist_ref, kernel_ref
    )


def add_block(total, kernel_ref, block_ref):
    for i in range(SHARDS):
        total = total + lax.dot_general(block_ref[i], kernel_ref[i], NT, preferred_element_type=F32)
    return total


def apply_first(kernel_ref, block_ref, total_ref):
    total_ref[...] = add_block(jnp.zeros(total_ref.shape, F32), kernel_ref, block_ref)


def apply_more(kernel_ref, before_ref, block_ref, total_ref):
    total_ref[...] = add_block(before_ref[...], kernel_ref, block_ref)


def apply_far(kernel_ref, before_ref, block_ref, total_ref):
    total_ref[...] = add_block(before_ref[:, WIDTH:], kernel_ref, block_ref)


def row_sum(product):
    ones = jnp.ones((8, WIDTH), F32)
    total = lax.dot_general(ones, product, NT, precision=lax.Precision.HIGHEST, preferred_element_type=F32)
    return total[:1]


def early_sums(first_ref, image_ref, sums_ref):
    first, image = first_ref[...], image_ref[...]
    sums_ref[0:1, :RHS] = row_sum(first * first)
    sums_ref[0:1, RHS:] = row_sum(first * image)
    sums_ref[1:2, :RHS] = row_sum(image * image)
    sums_ref[1:2, RHS:] = jnp.zeros((1, RHS), F32)


def late_sums(early_ref, noise_ref, first_ref, first_total_ref, image_ref, own_ref, peer_ref, second_ref, sums_ref):
    first, image = first_ref[...], image_ref[...]
    total = own_ref[:, :WIDTH] + peer_ref[...]
    second = noise_ref[...] * image + (first_total_ref[...] - total) * (1.0 / SIGMA)
    second_ref[...] = second
    sums_ref[0:2] = early_ref[...]
    sums_ref[2:3, :RHS] = row_sum(first * second)
    sums_ref[2:3, RHS:] = row_sum(image * second)
    sums_ref[3:4] = jnp.zeros((1, 2 * RHS), F32)


VMEM_LIMIT = pltpu.CompilerParams(vmem_limit_bytes=48 * 1024 * 1024)
SMEM = pl.BlockSpec(memory_space=pltpu.SMEM)
VMEM = pl.BlockSpec(memory_space=pltpu.VMEM)


def scratch(rows=2 * WIDTH):
    return [pltpu.VMEM((2, DEPTH, WIDTH), BF16), pltpu.VMEM((2, rows, WIDTH), F32)]


def shape(*dims, dtype=F32):
    return jax.ShapeDtypeStruct(dims, dtype)


def gathered(value, axes):
    count = math.prod(SIZES[AXES.index(axis)] for axis in axes)
    return lax.all_to_all(jnp.broadcast_to(value[None], (count,) + value.shape), axes, 0, 0)


def halo(block):
    first = [(i, i + 2 if i // 2 % 2 == 0 else i - 2) for i in range(N_BLK)]
    second = [(i, (i - 2 if i // 2 % 2 == 0 else i + 2) % N_BLK) for i in range(N_BLK)]
    fourth = [(i, (i - 4 if i % 2 == 0 else i + 4) % N_BLK) for i in range(N_BLK)]
    return tuple(lax.ppermute(block, BLK, route) for route in (first, second, fourth))


def kernel_shape(rows=2 * WIDTH):
    return shape(SHARDS, rows, WIDTH, dtype=BF16)


def call(body, out_shape, in_specs=None, scratch_shapes=()):
    extra = {} if in_specs is None else {"in_specs": in_specs}
    return pl.pallas_call(
        body, out_shape=out_shape, scratch_shapes=scratch_shapes, compiler_params=VMEM_LIMIT, **extra
    )


def body(points, lengthscale, noise_var, targets):
    coords = points / lengthscale[:, None] * UNIT
    message = jnp.concatenate(split(coords) + (targets.astype(BF16),), axis=0)
    block = gathered(message, ("x", "y_hi"))
    peer = lax.ppermute(message[: 2 * FEAT], "core", SWAP)
    *pairs, far = halo(block)

    near = lax.axis_index("z") % 2 == lax.axis_index("core")
    near_far = jnp.where(near, LEVELS[1], LEVELS[3]), jnp.where(near, LEVELS[3], LEVELS[1])
    weights, total, kernel_own = call(
        build_first,
        (shape(2 * WIDTH, DEPTH, dtype=BF16), shape(RHS, 2 * WIDTH), kernel_shape()),
        scratch_shapes=scratch(),
    )(message, peer, block)
    kernels = []
    for moved, level in zip(pairs, near_far):
        total, made = call(
            build_more,
            (shape(RHS, 2 * WIDTH), kernel_shape()),
            in_specs=[SMEM] + [VMEM] * 3,
            scratch_shapes=scratch(),
        )(jnp.stack([jnp.asarray(LEVELS[2], F32), level]), weights, total, moved)
        kernels.append(made)
    peer_total, kernel_far = call(
        build_far, (shape(RHS, WIDTH), kernel_shape(WIDTH)), scratch_shapes=scratch(WIDTH)
    )(weights, total, far)

    noise = noise_var[None, :]
    first_total = total[:, :WIDTH] + lax.ppermute(peer_total, "core", SWAP)
    image = noise * targets + first_total
    block = gathered((targets - SIGMA * image).astype(BF16), ("x", "y_hi"))
    *pairs, far = halo(block)
    early = call(early_sums, shape(2, 2 * RHS))(targets, image)
    total = call(apply_first, shape(RHS, 2 * WIDTH))(kernel_own, block)
    for made, moved in zip(kernels, pairs):
        total = call(apply_more, shape(RHS, 2 * WIDTH))(made, total, moved)
    peer_total = call(apply_far, shape(RHS, WIDTH))(kernel_far, total, far)
    peer_total = lax.ppermute(peer_total, "core", SWAP)
    second, sums = call(late_sums, (shape(RHS, WIDTH), shape(4, 2 * RHS)))(
        early, noise, targets, first_total, image, total, peer_total
    )
    for axes in (("x", "y_hi", "y_lo"), ("z", "core")):
        sums = jnp.sum(gathered(sums, axes), axis=0)

    (rr, rq), (qq, _), (rs, qs) = ((sums[i, :RHS], sums[i, RHS:]) for i in range(3))
    step = rr / rq
    norm_next = jnp.maximum(rr - 2.0 * step * rq + step * step * qq, 0.0)
    grown = 1.0 + norm_next / rr
    curvature = grown * grown * rq - step * grown * (qq + rs) + step * step * qs
    step_next = norm_next / curvature
    along = (step + step_next * grown)[:, None]
    across = (step_next * step)[:, None]
    solution = along * targets - across * image
    residual = targets - along * image + across * second
    return solution, residual


def solution(mesh):
    fine = Mesh(mesh.devices.reshape(SIZES), AXES)
    placed = (P(None, AXES), P(), P(AXES), P(None, AXES))
    return jax.shard_map(
        body, mesh=fine, in_specs=placed, out_specs=(P(None, AXES), P(None, AXES)), check_vma=False
    )
```

```python
import math

import jax
import jax.numpy as jnp
from jax import lax
from jax.experimental import pallas as pl
from jax.experimental.pallas import tpu as pltpu
from jax.sharding import Mesh, PartitionSpec as P

F32, BF16 = jnp.float32, jnp.bfloat16
AXES = ("y_lo", "z", "core", "x", "y_hi")
SIZES = (4, 8, 2, 4, 2)
BLK = ("y_lo", "z", "core")
N_BLK = 64

LN2 = math.log(2.0)
UNIT = math.sqrt(5.0) / LN2
SHIFT = 1.5 / LN2
OFFSET = 0.75 / LN2**2
LEVEL = math.log2(LN2**2 / 3.0) + SHIFT
LEVELS = tuple(LEVEL + math.log2(taper) for taper in (1.0, 0.75, 0.5, 0.25))
TINY = 1e-20

FEAT = 32
RHS = 64
WIDTH = 256
ROUGH = 80
DEPTH = 144
TOLD = 96
SHARDS = 8
SIGMA = 0.5
NT = (((1,), (1,)), ((), ()))


def prepare(points_ref, scale_ref, targets_ref, message_ref):
    row = lax.broadcasted_iota(jnp.int32, (FEAT, FEAT), 0)
    column = lax.broadcasted_iota(jnp.int32, (FEAT, FEAT), 1)
    scale = jnp.sum(jnp.where(row == column, scale_ref[...], 0.0), axis=1, keepdims=True)
    coords = points_ref[...] / scale * UNIT
    high = coords.astype(BF16)
    low = (coords - high.astype(F32)).astype(BF16)
    targets = targets_ref[...].astype(BF16)
    for i in range(SHARDS):
        message_ref[i, :FEAT] = high
        message_ref[i, FEAT:TOLD] = targets
        message_ref[i, TOLD:] = low


def square_rows(coords, first, second):
    squares = jnp.sum(coords * coords, axis=0, keepdims=True)
    one = squares.astype(BF16).astype(F32)
    two = (squares - one).astype(BF16).astype(F32)
    three = squares - one - two
    row = lax.broadcasted_iota(jnp.int32, (16, coords.shape[1]), 0)
    out = jnp.where((row >= second) & (row < second + 3), 1.0, 0.0)
    for at, piece in enumerate((one, two, three)):
        out = jnp.where(row == first + at, piece, out)
    return out.astype(BF16)


def build_shard(weights, levels, shard, cols_ref, dist_ref, kernel_ref):
    high = shard[:FEAT]
    coords = high.astype(F32)
    cols_ref[:FEAT] = high
    cols_ref[FEAT : 2 * FEAT] = high
    depth = ROUGH
    if shard.shape[0] > TOLD:
        low = shard[TOLD:]
        coords = coords + low.astype(F32)
        cols_ref[ROUGH : ROUGH + FEAT] = low
        cols_ref[ROUGH + FEAT :] = low
        depth = DEPTH
    cols_ref[2 * FEAT : ROUGH] = square_rows(coords, 0, 3)
    dist_ref[...] = jnp.dot(weights[:, :depth], cols_ref[:depth], preferred_element_type=F32)
    step = 64
    for half, level in enumerate(levels):
        for at in range(half * WIDTH, (half + 1) * WIDTH, step):
            part = jnp.maximum(dist_ref[at : at + step], TINY)
            moved = part * lax.rsqrt(part) + SHIFT
            entry = (moved * moved + OFFSET) * jnp.exp2(level - moved)
            kernel_ref[at : at + step] = entry.astype(BF16)
    return lax.dot_general(shard[FEAT:TOLD], kernel_ref[...], NT, preferred_element_type=F32)


def build_block(weights, levels, block_ref, cols_ref, dist_ref, kernel_ref):
    total = None
    for i in range(SHARDS):
        part = build_shard(weights, levels, block_ref[i], cols_ref.at[i % 2], dist_ref.at[i % 2], kernel_ref.at[i])
        total = part if total is None else total + part
    return total


def build_first(core_ref, both_ref, block_ref, weights_ref, total_ref, kernel_ref, cols_ref, dist_ref):
    for at, ref in enumerate((both_ref.at[core_ref[0]], both_ref.at[1 - core_ref[0]])):
        rows = slice(at * WIDTH, (at + 1) * WIDTH)
        high, low = ref[:FEAT].astype(F32), ref[FEAT:].astype(F32)
        extra = square_rows(high + low, 3, 0).astype(F32)
        halves = jnp.transpose(jnp.concatenate([-2.0 * high, -2.0 * low], axis=0)).astype(BF16)
        weights_ref[rows, : 2 * FEAT] = halves
        weights_ref[rows, 2 * FEAT : ROUGH] = jnp.transpose(extra).astype(BF16)
        weights_ref[rows, ROUGH:] = halves
    total_ref[...] = build_block(weights_ref[...], LEVELS[:2], block_ref, cols_ref, dist_ref, kernel_ref)


def build_more(level_ref, weights_ref, before_ref, block_ref, total_ref, kernel_ref, cols_ref, dist_ref):
    levels = (level_ref[0], level_ref[1])
    total_ref[...] = before_ref[...] + build_block(
        weights_ref[...], levels, block_ref, cols_ref, dist_ref, kernel_ref
    )


def build_far(weights_ref, before_ref, block_ref, total_ref, kernel_ref, cols_ref, dist_ref):
    total_ref[...] = before_ref[:, WIDTH:] + build_block(
        weights_ref[WIDTH:], LEVELS[3:], block_ref, cols_ref, dist_ref, kernel_ref
    )


def add_block(total, kernel_ref, block_ref):
    for i in range(SHARDS):
        total = total + lax.dot_general(block_ref[i], kernel_ref[i], NT, preferred_element_type=F32)
    return total


def apply_first(kernel_ref, block_ref, total_ref):
    total_ref[...] = add_block(jnp.zeros(total_ref.shape, F32), kernel_ref, block_ref)


def apply_more(kernel_ref, before_ref, block_ref, total_ref):
    total_ref[...] = add_block(before_ref[...], kernel_ref, block_ref)


def apply_far(kernel_ref, before_ref, block_ref, total_ref):
    total_ref[...] = add_block(before_ref[:, WIDTH:], kernel_ref, block_ref)


def row_sum(product):
    ones = jnp.ones((8, WIDTH), F32)
    total = lax.dot_general(ones, product, NT, precision=lax.Precision.HIGHEST, preferred_element_type=F32)
    return total[:1]


def early_sums(first_ref, image_ref, sums_ref):
    first, image = first_ref[...], image_ref[...]
    sums_ref[0:1, :RHS] = row_sum(first * first)
    sums_ref[0:1, RHS:] = row_sum(first * image)
    sums_ref[1:2, :RHS] = row_sum(image * image)
    sums_ref[1:2, RHS:] = jnp.zeros((1, RHS), F32)


def late_sums(
    core_ref, early_ref, noise_ref, first_ref, first_total_ref, image_ref, own_ref, both_ref, second_ref, sums_ref
):
    first, image = first_ref[...], image_ref[...]
    total = own_ref[:, :WIDTH] + both_ref[1 - core_ref[0]]
    second = noise_ref[...] * image + (first_total_ref[...] - total) * (1.0 / SIGMA)
    second_ref[...] = second
    sums_ref[0:2] = early_ref[...]
    sums_ref[2:3, :RHS] = row_sum(first * second)
    sums_ref[2:3, RHS:] = row_sum(image * second)
    sums_ref[3:4] = jnp.zeros((1, 2 * RHS), F32)


VMEM_LIMIT = pltpu.CompilerParams(vmem_limit_bytes=48 * 1024 * 1024)
SMEM = pl.BlockSpec(memory_space=pltpu.SMEM)
VMEM = pl.BlockSpec(memory_space=pltpu.VMEM)


def scratch(rows=2 * WIDTH):
    return [pltpu.VMEM((2, DEPTH, WIDTH), BF16), pltpu.VMEM((2, rows, WIDTH), F32)]


def shape(*dims, dtype=F32):
    return jax.ShapeDtypeStruct(dims, dtype)


def gathered(value, axes):
    count = math.prod(SIZES[AXES.index(axis)] for axis in axes)
    return lax.all_to_all(jnp.broadcast_to(value[None], (count,) + value.shape), axes, 0, 0)


def halo(block):
    first = [(i, i + 2 if i // 2 % 2 == 0 else i - 2) for i in range(N_BLK)]
    second = [(i, (i - 2 if i // 2 % 2 == 0 else i + 2) % N_BLK) for i in range(N_BLK)]
    fourth = [(i, (i - 4 if i % 2 == 0 else i + 4) % N_BLK) for i in range(N_BLK)]
    return tuple(lax.ppermute(block, BLK, route) for route in (first, second, fourth))


def kernel_shape(rows=2 * WIDTH):
    return shape(SHARDS, rows, WIDTH, dtype=BF16)


def call(body, out_shape, in_specs=None, scratch_shapes=()):
    extra = {} if in_specs is None else {"in_specs": in_specs}
    return pl.pallas_call(
        body, out_shape=out_shape, scratch_shapes=scratch_shapes, compiler_params=VMEM_LIMIT, **extra
    )


def body(points, lengthscale, noise_var, targets):
    core = lax.axis_index("core")
    which = core.astype(jnp.int32).reshape(1)
    message = call(prepare, shape(SHARDS, 2 * FEAT + RHS, WIDTH, dtype=BF16))(points, lengthscale[None, :], targets)
    coords = jnp.concatenate([message[0, :FEAT], message[0, TOLD:]], axis=0)
    both = lax.all_gather(coords, "core")
    block = lax.all_to_all(message, ("x", "y_hi"), 0, 0)
    *pairs, far = halo(block[:, :TOLD])

    near = lax.axis_index("z") % 2 == core
    near_far = jnp.where(near, LEVELS[1], LEVELS[3]), jnp.where(near, LEVELS[3], LEVELS[1])
    weights, total, kernel_own = call(
        build_first,
        (shape(2 * WIDTH, DEPTH, dtype=BF16), shape(RHS, 2 * WIDTH), kernel_shape()),
        in_specs=[SMEM] + [VMEM] * 2,
        scratch_shapes=scratch(),
    )(which, both, block)
    kernels = []
    for moved, level in zip(pairs, near_far):
        total, made = call(
            build_more,
            (shape(RHS, 2 * WIDTH), kernel_shape()),
            in_specs=[SMEM] + [VMEM] * 3,
            scratch_shapes=scratch(),
        )(jnp.stack([jnp.asarray(LEVELS[2], F32), level]), weights, total, moved)
        kernels.append(made)
    peer_total, kernel_far = call(
        build_far, (shape(RHS, WIDTH), kernel_shape(WIDTH)), scratch_shapes=scratch(WIDTH)
    )(weights, total, far)

    noise = noise_var[None, :]
    both = lax.all_gather(peer_total, "core")
    first_total = total[:, :WIDTH] + jnp.where(core == 0, both[1], both[0])
    image = noise * targets + first_total
    block = gathered((targets - SIGMA * image).astype(BF16), ("x", "y_hi"))
    *pairs, far = halo(block)
    early = call(early_sums, shape(2, 2 * RHS))(targets, image)
    total = call(apply_first, shape(RHS, 2 * WIDTH))(kernel_own, block)
    for made, moved in zip(kernels, pairs):
        total = call(apply_more, shape(RHS, 2 * WIDTH))(made, total, moved)
    peer_total = call(apply_far, shape(RHS, WIDTH))(kernel_far, total, far)
    both = lax.all_gather(peer_total, "core")
    second, sums = call(
        late_sums, (shape(RHS, WIDTH), shape(4, 2 * RHS)), in_specs=[SMEM] + [VMEM] * 7
    )(which, early, noise, targets, first_total, image, total, both)
    for axes in (("x", "y_hi", "y_lo"), ("z", "core")):
        sums = jnp.sum(gathered(sums, axes), axis=0)

    (rr, rq), (qq, _), (rs, qs) = ((sums[i, :RHS], sums[i, RHS:]) for i in range(3))
    step = rr / rq
    norm_next = jnp.maximum(rr - 2.0 * step * rq + step * step * qq, 0.0)
    grown = 1.0 + norm_next / rr
    curvature = grown * grown * rq - step * grown * (qq + rs) + step * step * qs
    step_next = norm_next / curvature
    along = (step + step_next * grown)[:, None]
    across = (step_next * step)[:, None]
    solution = along * targets - across * image
    residual = targets - along * image + across * second
    return solution, residual


def solution(mesh):
    fine = Mesh(mesh.devices.reshape(SIZES), AXES)
    placed = (P(None, AXES), P(), P(AXES), P(None, AXES))
    return jax.shard_map(
        body, mesh=fine, in_specs=placed, out_specs=(P(None, AXES), P(None, AXES)), check_vma=False
    )
```

```python
import functools
import math

import jax
import jax.numpy as jnp
from jax import lax
from jax.experimental import pallas as pl
from jax.experimental.pallas import tpu as pltpu
from jax.sharding import Mesh, PartitionSpec as P

F32, BF16 = jnp.float32, jnp.bfloat16
AXES = ("y_lo", "z", "core", "x", "y_hi")
SIZES = (4, 8, 2, 4, 2)
BLK = ("y_lo", "z", "core")
N_BLK = 64

LN2 = math.log(2.0)
UNIT = math.sqrt(5.0) / LN2
SHIFT = 1.5 / LN2
OFFSET = 0.75 / LN2**2
LEVEL = math.log2(LN2**2 / 3.0) + SHIFT
LEVELS = tuple(LEVEL + math.log2(taper) for taper in (1.0, 0.75, 0.5, 0.25))
TINY = 1e-20

FEAT = 32
RHS = 64
WIDTH = 256
ROUGH = 80
DEPTH = 144
TOLD = 96
SHARDS = 8
SIGMA = 0.5
NT = (((1,), (1,)), ((), ()))


def square_rows(coords, first, second):
    squares = jnp.sum(coords * coords, axis=0, keepdims=True)
    one = squares.astype(BF16).astype(F32)
    two = (squares - one).astype(BF16).astype(F32)
    three = squares - one - two
    row = lax.broadcasted_iota(jnp.int32, (16, coords.shape[1]), 0)
    out = jnp.where((row >= second) & (row < second + 3), 1.0, 0.0)
    for at, piece in enumerate((one, two, three)):
        out = jnp.where(row == first + at, piece, out)
    return out.astype(BF16)


def build_shard(weights, levels, shard, cols_ref, dist_ref, kernel_ref):
    high = shard[:FEAT]
    coords = high.astype(F32)
    cols_ref[:FEAT] = high
    cols_ref[FEAT : 2 * FEAT] = high
    depth = ROUGH
    if shard.shape[0] > TOLD:
        low = shard[TOLD:]
        coords = coords + low.astype(F32)
        cols_ref[ROUGH : ROUGH + FEAT] = low
        cols_ref[ROUGH + FEAT :] = low
        depth = DEPTH
    cols_ref[2 * FEAT : ROUGH] = square_rows(coords, 0, 3)
    dist_ref[...] = jnp.dot(weights[:, :depth], cols_ref[:depth], preferred_element_type=F32)
    step = 64
    for half, level in enumerate(levels):
        for at in range(half * WIDTH, (half + 1) * WIDTH, step):
            part = jnp.maximum(dist_ref[at : at + step], TINY)
            moved = part * lax.rsqrt(part) + SHIFT
            entry = (moved * moved + OFFSET) * jnp.exp2(level - moved)
            kernel_ref[at : at + step] = entry.astype(BF16)
    return lax.dot_general(shard[FEAT:TOLD], kernel_ref[...], NT, preferred_element_type=F32)


def build_block(weights, levels, block_ref, cols_ref, dist_ref, kernel_ref):
    total = None
    for i in range(SHARDS):
        part = build_shard(weights, levels, block_ref[i], cols_ref.at[i % 2], dist_ref.at[i % 2], kernel_ref.at[i])
        total = part if total is None else total + part
    return total


def build_first(both_ref, block_ref, weights_ref, own_ref, peer_ref, kernel_ref, cols_ref, dist_ref):
    core = lax.axis_index("core")
    for at, ref in enumerate((both_ref.at[core], both_ref.at[1 - core])):
        rows = slice(at * WIDTH, (at + 1) * WIDTH)
        high, low = ref[:FEAT].astype(F32), ref[FEAT:].astype(F32)
        extra = square_rows(high + low, 3, 0).astype(F32)
        halves = jnp.transpose(jnp.concatenate([-2.0 * high, -2.0 * low], axis=0)).astype(BF16)
        weights_ref[rows, : 2 * FEAT] = halves
        weights_ref[rows, 2 * FEAT : ROUGH] = jnp.transpose(extra).astype(BF16)
        weights_ref[rows, ROUGH:] = halves
    total = build_block(weights_ref[...], LEVELS[:2], block_ref, cols_ref, dist_ref, kernel_ref)
    own_ref[...] = total[:, :WIDTH]
    peer_ref[...] = total[:, WIDTH:]


def build_far(weights_ref, before_ref, block_ref, peer_ref, kernel_ref, cols_ref, dist_ref):
    peer_ref[...] = before_ref[...] + build_block(
        weights_ref[WIDTH:], LEVELS[3:], block_ref, cols_ref, dist_ref, kernel_ref
    )


def build_pair(
    second, weights_ref, own_before, peer_before, block_ref, own_ref, peer_ref, kernel_ref, cols_ref, dist_ref
):
    near = (lax.axis_index("z") + lax.axis_index("core") + second) % 2 == 0
    levels = LEVELS[2], jnp.where(near, LEVELS[1], LEVELS[3])
    total = build_block(weights_ref[...], levels, block_ref, cols_ref, dist_ref, kernel_ref)
    own_ref[...] = own_before[...] + total[:, :WIDTH]
    peer_ref[...] = peer_before[...] + total[:, WIDTH:]


def apply_block(kernel_ref, block_ref):
    total = None
    for i in range(SHARDS):
        part = lax.dot_general(block_ref[i], kernel_ref[i], NT, preferred_element_type=F32)
        total = part if total is None else total + part
    return total


def apply_first(kernel_ref, block_ref, own_ref, peer_ref):
    total = apply_block(kernel_ref, block_ref)
    own_ref[...] = total[:, :WIDTH]
    peer_ref[...] = total[:, WIDTH:]


def apply_far(kernel_ref, before_ref, block_ref, peer_ref):
    peer_ref[...] = before_ref[...] + apply_block(kernel_ref, block_ref)


def apply_pair(kernel_ref, own_before, peer_before, block_ref, own_ref, peer_ref):
    total = apply_block(kernel_ref, block_ref)
    own_ref[...] = own_before[...] + total[:, :WIDTH]
    peer_ref[...] = peer_before[...] + total[:, WIDTH:]


def row_sum(product):
    ones = jnp.ones((8, WIDTH), F32)
    total = lax.dot_general(ones, product, NT, precision=lax.Precision.HIGHEST, preferred_element_type=F32)
    return total[:1]


def early_sums(first_ref, image_ref, sums_ref):
    first, image = first_ref[...], image_ref[...]
    sums_ref[0:1, :RHS] = row_sum(first * first)
    sums_ref[0:1, RHS:] = row_sum(first * image)
    sums_ref[1:2, :RHS] = row_sum(image * image)
    sums_ref[1:2, RHS:] = jnp.zeros((1, RHS), F32)


def late_sums(
    early_ref, noise_ref, first_ref, first_total_ref, image_ref, own_ref, both_ref, second_ref, sums_ref
):
    first, image = first_ref[...], image_ref[...]
    total = own_ref[...] + both_ref[1 - lax.axis_index("core")]
    second = noise_ref[...] * image + (first_total_ref[...] - total) * (1.0 / SIGMA)
    second_ref[...] = second
    sums_ref[0:2] = early_ref[...]
    sums_ref[2:3, :RHS] = row_sum(first * second)
    sums_ref[2:3, RHS:] = row_sum(image * second)
    sums_ref[3:4] = jnp.zeros((1, 2 * RHS), F32)


VMEM_LIMIT = pltpu.CompilerParams(vmem_limit_bytes=48 * 1024 * 1024)


def scratch(rows=2 * WIDTH):
    return [pltpu.VMEM((2, DEPTH, WIDTH), BF16), pltpu.VMEM((2, rows, WIDTH), F32)]


def shape(*dims, dtype=F32):
    return jax.ShapeDtypeStruct(dims, dtype)


def gathered(value, axes):
    count = math.prod(SIZES[AXES.index(axis)] for axis in axes)
    return lax.all_to_all(jnp.broadcast_to(value[None], (count,) + value.shape), axes, 0, 0)


def halo(block):
    first = [(i, i + 2 if i // 2 % 2 == 0 else i - 2) for i in range(N_BLK)]
    second = [(i, (i - 2 if i // 2 % 2 == 0 else i + 2) % N_BLK) for i in range(N_BLK)]
    fourth = [(i, (i - 4 if i % 2 == 0 else i + 4) % N_BLK) for i in range(N_BLK)]
    return tuple(lax.ppermute(block, BLK, route) for route in (fourth, first, second))


def kernel_shape(rows=2 * WIDTH):
    return shape(SHARDS, rows, WIDTH, dtype=BF16)


def call(body, out_shape, scratch_shapes=()):
    return pl.pallas_call(body, out_shape=out_shape, scratch_shapes=scratch_shapes, compiler_params=VMEM_LIMIT)


def body(points, lengthscale, noise_var, targets):
    coords = points / lengthscale[:, None] * UNIT
    high = lax.reduce_precision(coords, 8, 7)
    message = jnp.concatenate([high, targets, coords - high], axis=0).astype(BF16)
    coords = jnp.concatenate([message[:FEAT], message[TOLD:]], axis=0)
    both = lax.all_gather(coords, "core")
    block = gathered(message, ("x", "y_hi"))
    far, *pairs = halo(block[:, :TOLD])

    half = shape(RHS, WIDTH)
    weights, own, peer, kernel_own = call(
        build_first,
        (shape(2 * WIDTH, DEPTH, dtype=BF16), half, half, kernel_shape()),
        scratch_shapes=scratch(),
    )(both, block)
    peer, kernel_far = call(build_far, (half, kernel_shape(WIDTH)), scratch_shapes=scratch(WIDTH))(weights, peer, far)
    kernels = []
    for second, moved in enumerate(pairs):
        own, peer, made = call(
            functools.partial(build_pair, second), (half, half, kernel_shape()), scratch_shapes=scratch()
        )(weights, own, peer, moved)
        kernels.append(made)

    noise = noise_var[None, :]
    both = lax.all_gather(peer, "core")
    first_total = own + jnp.where(lax.axis_index("core") == 0, both[1], both[0])
    image = noise * targets + first_total
    block = gathered((targets - SIGMA * image).astype(BF16), ("x", "y_hi"))
    far, *pairs = halo(block)
    early = call(early_sums, shape(2, 2 * RHS))(targets, image)
    own, peer = call(apply_first, (half, half))(kernel_own, block)
    peer = call(apply_far, half)(kernel_far, peer, far)
    for made, moved in zip(kernels, pairs):
        own, peer = call(apply_pair, (half, half))(made, own, peer, moved)
    both = lax.all_gather(peer, "core")
    second, sums = call(late_sums, (half, shape(4, 2 * RHS)))(
        early, noise, targets, first_total, image, own, both
    )
    for axes in (("x", "y_hi", "y_lo"), ("z", "core")):
        sums = jnp.sum(gathered(sums, axes), axis=0)

    (rr, rq), (qq, _), (rs, qs) = ((sums[i, :RHS], sums[i, RHS:]) for i in range(3))
    step = rr / rq
    norm_next = jnp.maximum(rr - 2.0 * step * rq + step * step * qq, 0.0)
    grown = 1.0 + norm_next / rr
    curvature = grown * grown * rq - step * grown * (qq + rs) + step * step * qs
    step_next = norm_next / curvature
    along = (step + step_next * grown)[:, None]
    across = (step_next * step)[:, None]
    solution = along * targets - across * image
    residual = targets - along * image + across * second
    return solution, residual


def solution(mesh):
    fine = Mesh(mesh.devices.reshape(SIZES), AXES)
    placed = (P(None, AXES), P(), P(AXES), P(None, AXES))
    return jax.shard_map(
        body, mesh=fine, in_specs=placed, out_specs=(P(None, AXES), P(None, AXES)), check_vma=False
    )
```

```python
import functools
import math

import jax
import jax.numpy as jnp
from jax import lax
from jax.experimental import pallas as pl
from jax.experimental.pallas import tpu as pltpu
from jax.sharding import Mesh, PartitionSpec as P

F32, BF16 = jnp.float32, jnp.bfloat16
AXES = ("y_lo", "z", "core", "x", "y_hi")
SIZES = (4, 8, 2, 4, 2)
BLK = ("y_lo", "z", "core")
N_BLK = 64

LN2 = math.log(2.0)
UNIT = math.sqrt(5.0) / LN2
GRID = 2.0 / 1.5
SPAN = UNIT / GRID
SHIFT = 1.5 / LN2
OFFSET = 0.75 / LN2**2
LEVEL = math.log2(LN2**2 / 3.0) + SHIFT
LEVELS = tuple(LEVEL + math.log2(taper) for taper in (1.0, 0.75, 0.5, 0.25))
TINY = 1e-20

FEAT = 32
RHS = 64
WIDTH = 256
DEPTH = 80
SHARDS = 8
SIGMA = 0.5
NT = (((1,), (1,)), ((), ()))


def square_rows(coords, first, second):
    squares = jnp.sum(coords * coords, axis=0, keepdims=True) * SPAN**2
    one = squares.astype(BF16).astype(F32)
    two = (squares - one).astype(BF16).astype(F32)
    three = squares - one - two
    row = lax.broadcasted_iota(jnp.int32, (16, coords.shape[1]), 0)
    out = jnp.where((row >= second) & (row < second + 3), 1.0, 0.0)
    for at, piece in enumerate((one, two, three)):
        out = jnp.where(row == first + at, piece, out)
    return out


def build_shard(weights, levels, shard, cols_ref, dist_ref, kernel_ref):
    coords = shard[:FEAT]
    cols_ref[:FEAT] = coords
    cols_ref[FEAT : 2 * FEAT] = coords
    cols_ref[2 * FEAT :] = square_rows(coords.astype(F32), 0, 3).astype(BF16)
    dist_ref[...] = jnp.dot(weights, cols_ref[...], preferred_element_type=F32)
    step = 64
    for half, level in enumerate(levels):
        for at in range(half * WIDTH, (half + 1) * WIDTH, step):
            part = jnp.maximum(dist_ref[at : at + step], TINY)
            moved = part * lax.rsqrt(part) + SHIFT
            entry = (moved * moved + OFFSET) * jnp.exp2(level - moved)
            kernel_ref[at : at + step] = entry.astype(BF16)
    return lax.dot_general(shard[FEAT:], kernel_ref[...], NT, preferred_element_type=F32)


def build_block(weights, levels, block_ref, cols_ref, dist_ref, kernel_ref):
    total = None
    for i in range(SHARDS):
        part = build_shard(weights, levels, block_ref[i], cols_ref.at[i % 2], dist_ref.at[i % 2], kernel_ref.at[i])
        total = part if total is None else total + part
    return total


def build_first(both_ref, block_ref, weights_ref, own_ref, peer_ref, kernel_ref, cols_ref, dist_ref):
    core = lax.axis_index("core")
    for at, ref in enumerate((both_ref.at[core], both_ref.at[1 - core])):
        rows = slice(at * WIDTH, (at + 1) * WIDTH)
        coords = ref[...]
        scaled = coords * (-2.0 * SPAN**2)
        high = scaled.astype(BF16).astype(F32)
        stacked = jnp.concatenate([high, scaled - high, square_rows(coords, 3, 0)], axis=0)
        weights_ref[rows] = jnp.transpose(stacked).astype(BF16)
    total = build_block(weights_ref[...], LEVELS[:2], block_ref, cols_ref, dist_ref, kernel_ref)
    own_ref[...] = total[:, :WIDTH]
    peer_ref[...] = total[:, WIDTH:]


def build_far(weights_ref, before_ref, block_ref, peer_ref, kernel_ref, cols_ref, dist_ref):
    peer_ref[...] = before_ref[...] + build_block(
        weights_ref[WIDTH:], LEVELS[3:], block_ref, cols_ref, dist_ref, kernel_ref
    )


def build_pair(
    second, weights_ref, own_before, peer_before, block_ref, own_ref, peer_ref, kernel_ref, cols_ref, dist_ref
):
    near = (lax.axis_index("z") + lax.axis_index("core") + second) % 2 == 0
    levels = LEVELS[2], jnp.where(near, LEVELS[1], LEVELS[3])
    total = build_block(weights_ref[...], levels, block_ref, cols_ref, dist_ref, kernel_ref)
    own_ref[...] = own_before[...] + total[:, :WIDTH]
    peer_ref[...] = peer_before[...] + total[:, WIDTH:]


def apply_block(kernel_ref, block_ref):
    total = None
    for i in range(SHARDS):
        part = lax.dot_general(block_ref[i], kernel_ref[i], NT, preferred_element_type=F32)
        total = part if total is None else total + part
    return total


def apply_first(kernel_ref, block_ref, own_ref, peer_ref):
    total = apply_block(kernel_ref, block_ref)
    own_ref[...] = total[:, :WIDTH]
    peer_ref[...] = total[:, WIDTH:]


def apply_far(kernel_ref, before_ref, block_ref, peer_ref):
    peer_ref[...] = before_ref[...] + apply_block(kernel_ref, block_ref)


def apply_pair(kernel_ref, own_before, peer_before, block_ref, own_ref, peer_ref):
    total = apply_block(kernel_ref, block_ref)
    own_ref[...] = own_before[...] + total[:, :WIDTH]
    peer_ref[...] = peer_before[...] + total[:, WIDTH:]


def row_sum(product):
    ones = jnp.ones((8, WIDTH), F32)
    total = lax.dot_general(ones, product, NT, precision=lax.Precision.HIGHEST, preferred_element_type=F32)
    return total[:1]


def early_sums(first_ref, image_ref, sums_ref):
    first, image = first_ref[...], image_ref[...]
    sums_ref[0:1, :RHS] = row_sum(first * first)
    sums_ref[0:1, RHS:] = row_sum(first * image)
    sums_ref[1:2, :RHS] = row_sum(image * image)
    sums_ref[1:2, RHS:] = jnp.zeros((1, RHS), F32)


def late_sums(
    early_ref, noise_ref, first_ref, first_total_ref, image_ref, own_ref, both_ref, second_ref, sums_ref
):
    first, image = first_ref[...], image_ref[...]
    total = own_ref[...] + both_ref[1 - lax.axis_index("core")]
    second = noise_ref[...] * image + (first_total_ref[...] - total) * (1.0 / SIGMA)
    second_ref[...] = second
    sums_ref[0:2] = early_ref[...]
    sums_ref[2:3, :RHS] = row_sum(first * second)
    sums_ref[2:3, RHS:] = row_sum(image * second)
    sums_ref[3:4] = jnp.zeros((1, 2 * RHS), F32)


VMEM_LIMIT = pltpu.CompilerParams(vmem_limit_bytes=48 * 1024 * 1024)


def scratch(rows=2 * WIDTH):
    return [pltpu.VMEM((2, DEPTH, WIDTH), BF16), pltpu.VMEM((2, rows, WIDTH), F32)]


def shape(*dims, dtype=F32):
    return jax.ShapeDtypeStruct(dims, dtype)


def gathered(value, axes):
    count = math.prod(SIZES[AXES.index(axis)] for axis in axes)
    return lax.all_to_all(jnp.broadcast_to(value[None], (count,) + value.shape), axes, 0, 0)


def halo(block):
    first = [(i, i + 2 if i // 2 % 2 == 0 else i - 2) for i in range(N_BLK)]
    second = [(i, (i - 2 if i // 2 % 2 == 0 else i + 2) % N_BLK) for i in range(N_BLK)]
    fourth = [(i, (i - 4 if i % 2 == 0 else i + 4) % N_BLK) for i in range(N_BLK)]
    return tuple(lax.ppermute(block, BLK, route) for route in (fourth, first, second))


def kernel_shape(rows=2 * WIDTH):
    return shape(SHARDS, rows, WIDTH, dtype=BF16)


def call(body, out_shape, scratch_shapes=()):
    return pl.pallas_call(body, out_shape=out_shape, scratch_shapes=scratch_shapes, compiler_params=VMEM_LIMIT)


def body(points, lengthscale, noise_var, targets):
    coords = points / lengthscale[:, None] * GRID
    both = lax.all_gather(coords, "core")
    block = gathered(jnp.concatenate([coords, targets], axis=0).astype(BF16), ("x", "y_hi"))
    far, *pairs = halo(block)

    half = shape(RHS, WIDTH)
    weights, own, peer, kernel_own = call(
        build_first,
        (shape(2 * WIDTH, DEPTH, dtype=BF16), half, half, kernel_shape()),
        scratch_shapes=scratch(),
    )(both, block)
    peer, kernel_far = call(build_far, (half, kernel_shape(WIDTH)), scratch_shapes=scratch(WIDTH))(weights, peer, far)
    kernels = []
    for second, moved in enumerate(pairs):
        own, peer, made = call(
            functools.partial(build_pair, second), (half, half, kernel_shape()), scratch_shapes=scratch()
        )(weights, own, peer, moved)
        kernels.append(made)

    noise = noise_var[None, :]
    both = lax.all_gather(peer, "core")
    first_total = own + jnp.where(lax.axis_index("core") == 0, both[1], both[0])
    image = noise * targets + first_total
    block = gathered((targets - SIGMA * image).astype(BF16), ("x", "y_hi"))
    far, *pairs = halo(block)
    early = call(early_sums, shape(2, 2 * RHS))(targets, image)
    own, peer = call(apply_first, (half, half))(kernel_own, block)
    peer = call(apply_far, half)(kernel_far, peer, far)
    for made, moved in zip(kernels, pairs):
        own, peer = call(apply_pair, (half, half))(made, own, peer, moved)
    both = lax.all_gather(peer, "core")
    second, sums = call(late_sums, (half, shape(4, 2 * RHS)))(
        early, noise, targets, first_total, image, own, both
    )
    for axes in (("x", "y_hi", "y_lo"), ("z", "core")):
        sums = jnp.sum(gathered(sums, axes), axis=0)

    (rr, rq), (qq, _), (rs, qs) = ((sums[i, :RHS], sums[i, RHS:]) for i in range(3))
    step = rr / rq
    norm_next = jnp.maximum(rr - 2.0 * step * rq + step * step * qq, 0.0)
    grown = 1.0 + norm_next / rr
    curvature = grown * grown * rq - step * grown * (qq + rs) + step * step * qs
    step_next = norm_next / curvature
    along = (step + step_next * grown)[:, None]
    across = (step_next * step)[:, None]
    solution = along * targets - across * image
    residual = targets - along * image + across * second
    return solution, residual


def solution(mesh):
    fine = Mesh(mesh.devices.reshape(SIZES), AXES)
    placed = (P(None, AXES), P(), P(AXES), P(None, AXES))
    return jax.shard_map(
        body, mesh=fine, in_specs=placed, out_specs=(P(None, AXES), P(None, AXES)), check_vma=False
    )
```

```python
import functools
import math

import jax
import jax.numpy as jnp
from jax import lax
from jax.experimental import pallas as pl
from jax.experimental.pallas import tpu as pltpu
from jax.sharding import Mesh, PartitionSpec as P

F32, BF16 = jnp.float32, jnp.bfloat16
AXES = ("y_lo", "z", "core", "x", "y_hi")
SIZES = (4, 8, 2, 4, 2)
BLK = ("y_lo", "z", "core")
N_BLK = 64

LN2 = math.log(2.0)
UNIT = math.sqrt(5.0) / LN2
GRID = 2.0 / 1.5
SPAN = UNIT / GRID
SHIFT = 1.5 / LN2
OFFSET = 0.75 / LN2**2
LEVEL = math.log2(LN2**2 / 3.0) + SHIFT
LEVELS = tuple(LEVEL + math.log2(taper) for taper in (1.0, 0.75, 0.5, 0.25))
TINY = 1e-20

FEAT = 32
RHS = 64
WIDTH = 256
DEPTH = 80
SHARDS = 8
SIGMA = 0.5
NT = (((1,), (1,)), ((), ()))


def square_rows(coords, first, second):
    squares = jnp.sum(coords * coords, axis=0, keepdims=True) * SPAN**2
    one = squares.astype(BF16).astype(F32)
    two = (squares - one).astype(BF16).astype(F32)
    three = squares - one - two
    row = lax.broadcasted_iota(jnp.int32, (16, coords.shape[1]), 0)
    out = jnp.where((row >= second) & (row < second + 3), 1.0, 0.0)
    for at, piece in enumerate((one, two, three)):
        out = jnp.where(row == first + at, piece, out)
    return out


def build_shard(weights, levels, shard, cols_ref, dist_ref, kernel_ref):
    coords = shard[:FEAT]
    cols_ref[:FEAT] = coords
    cols_ref[FEAT : 2 * FEAT] = coords
    cols_ref[2 * FEAT :] = square_rows(coords.astype(F32), 0, 3).astype(BF16)
    dist_ref[...] = jnp.dot(weights, cols_ref[...], preferred_element_type=F32)
    step = 64
    for half, level in enumerate(levels):
        for at in range(half * WIDTH, (half + 1) * WIDTH, step):
            part = jnp.maximum(dist_ref[at : at + step], TINY)
            moved = part * lax.rsqrt(part) + SHIFT
            entry = (moved * moved + OFFSET) * jnp.exp2(level - moved)
            kernel_ref[at : at + step] = entry.astype(BF16)
    return lax.dot_general(shard[FEAT:], kernel_ref[...], NT, preferred_element_type=F32)


def build_block(weights, levels, block_ref, cols_ref, dist_ref, kernel_ref):
    total = None
    for i in range(SHARDS):
        part = build_shard(weights, levels, block_ref[i], cols_ref.at[i % 2], dist_ref.at[i % 2], kernel_ref.at[i])
        total = part if total is None else total + part
    return total


def build_first(scale_ref, both_ref, block_ref, weights_ref, own_ref, peer_ref, kernel_ref, cols_ref, dist_ref):
    core = lax.axis_index("core")
    row = lax.broadcasted_iota(jnp.int32, (FEAT, FEAT), 0)
    column = lax.broadcasted_iota(jnp.int32, (FEAT, FEAT), 1)
    scale = jnp.sum(jnp.where(row == column, scale_ref[:, :FEAT], 0.0), axis=1, keepdims=True)
    for at, ref in enumerate((both_ref.at[core], both_ref.at[1 - core])):
        rows = slice(at * WIDTH, (at + 1) * WIDTH)
        coords = ref[...] * scale
        scaled = coords * (-2.0 * SPAN**2)
        high = scaled.astype(BF16).astype(F32)
        stacked = jnp.concatenate([high, scaled - high, square_rows(coords, 3, 0)], axis=0)
        weights_ref[rows] = jnp.transpose(stacked).astype(BF16)
    total = build_block(weights_ref[...], LEVELS[:2], block_ref, cols_ref, dist_ref, kernel_ref)
    own_ref[...] = total[:, :WIDTH]
    peer_ref[...] = total[:, WIDTH:]


def build_far(weights_ref, before_ref, block_ref, peer_ref, kernel_ref, cols_ref, dist_ref):
    peer_ref[...] = before_ref[...] + build_block(
        weights_ref[WIDTH:], LEVELS[3:], block_ref, cols_ref, dist_ref, kernel_ref
    )


def build_pair(
    second, weights_ref, own_before, peer_before, block_ref, own_ref, peer_ref, kernel_ref, cols_ref, dist_ref
):
    near = (lax.axis_index("z") + lax.axis_index("core") + second) % 2 == 0
    levels = LEVELS[2], jnp.where(near, LEVELS[1], LEVELS[3])
    total = build_block(weights_ref[...], levels, block_ref, cols_ref, dist_ref, kernel_ref)
    own_ref[...] = own_before[...] + total[:, :WIDTH]
    peer_ref[...] = peer_before[...] + total[:, WIDTH:]


def apply_block(kernel_ref, block_ref):
    total = None
    for i in range(SHARDS):
        part = lax.dot_general(block_ref[i], kernel_ref[i], NT, preferred_element_type=F32)
        total = part if total is None else total + part
    return total


def apply_first(kernel_ref, block_ref, own_ref, peer_ref):
    total = apply_block(kernel_ref, block_ref)
    own_ref[...] = total[:, :WIDTH]
    peer_ref[...] = total[:, WIDTH:]


def apply_far(kernel_ref, before_ref, block_ref, peer_ref):
    peer_ref[...] = before_ref[...] + apply_block(kernel_ref, block_ref)


def apply_pair(kernel_ref, own_before, peer_before, block_ref, own_ref, peer_ref):
    total = apply_block(kernel_ref, block_ref)
    own_ref[...] = own_before[...] + total[:, :WIDTH]
    peer_ref[...] = peer_before[...] + total[:, WIDTH:]


def row_sum(product):
    ones = jnp.ones((8, WIDTH), F32)
    total = lax.dot_general(ones, product, NT, precision=lax.Precision.HIGHEST, preferred_element_type=F32)
    return total[:1]


def early_sums(first_ref, image_ref, sums_ref):
    first, image = first_ref[...], image_ref[...]
    sums_ref[0:1, :RHS] = row_sum(first * first)
    sums_ref[0:1, RHS:] = row_sum(first * image)
    sums_ref[1:2, :RHS] = row_sum(image * image)
    sums_ref[1:2, RHS:] = jnp.zeros((1, RHS), F32)


def late_sums(
    early_ref, noise_ref, images_ref, first_ref, image_ref, first_total_ref, own_ref, peer_ref, sums_ref
):
    core = lax.axis_index("core")
    image = image_ref[...]
    known = noise_ref[...] * image + (first_total_ref[...] - own_ref[...]) * (1.0 / SIGMA)
    lent = peer_ref[...] * (1.0 / SIGMA)
    sums_ref[0:2] = early_ref[...]
    sums_ref[2:3, :RHS] = row_sum(first_ref[...] * known - images_ref[1 - core, :RHS] * lent)
    sums_ref[2:3, RHS:] = row_sum(image * known - images_ref[1 - core, RHS:] * lent)
    sums_ref[3:4] = jnp.zeros((1, 2 * RHS), F32)


VMEM_LIMIT = pltpu.CompilerParams(vmem_limit_bytes=48 * 1024 * 1024)


def scratch(rows=2 * WIDTH):
    return [pltpu.VMEM((2, DEPTH, WIDTH), BF16), pltpu.VMEM((2, rows, WIDTH), F32)]


def shape(*dims, dtype=F32):
    return jax.ShapeDtypeStruct(dims, dtype)


def gathered(value, axes):
    count = math.prod(SIZES[AXES.index(axis)] for axis in axes)
    return lax.all_to_all(jnp.broadcast_to(value[None], (count,) + value.shape), axes, 0, 0)


def halo(block):
    first = [(i, i + 2 if i // 2 % 2 == 0 else i - 2) for i in range(N_BLK)]
    second = [(i, (i - 2 if i // 2 % 2 == 0 else i + 2) % N_BLK) for i in range(N_BLK)]
    fourth = [(i, (i - 4 if i % 2 == 0 else i + 4) % N_BLK) for i in range(N_BLK)]
    return tuple(lax.ppermute(block, BLK, route) for route in (fourth, first, second))


def kernel_shape(rows=2 * WIDTH):
    return shape(SHARDS, rows, WIDTH, dtype=BF16)


def call(body, out_shape, scratch_shapes=()):
    return pl.pallas_call(body, out_shape=out_shape, scratch_shapes=scratch_shapes, compiler_params=VMEM_LIMIT)


def body(points, lengthscale, noise_var, targets):
    scale = GRID / jnp.pad(lengthscale, (0, RHS), constant_values=GRID)
    exact = jnp.concatenate([points, targets], axis=0) * scale[:, None]
    block = gathered(exact.astype(BF16), ("x", "y_hi"))
    both = lax.all_gather(points, "core")
    far, *pairs = halo(block)

    half = shape(RHS, WIDTH)
    weights, own, peer, kernel_own = call(
        build_first,
        (shape(2 * WIDTH, DEPTH, dtype=BF16), half, half, kernel_shape()),
        scratch_shapes=scratch(),
    )(scale[None], both, block)
    kernels = {}
    for kind in "ABF":
        if kind == "F":
            peer, kernels[kind] = call(build_far, (half, kernel_shape(WIDTH)), scratch_shapes=scratch(WIDTH))(
                weights, peer, far
            )
        else:
            second = "AB".index(kind)
            own, peer, kernels[kind] = call(
                functools.partial(build_pair, second), (half, half, kernel_shape()), scratch_shapes=scratch()
            )(weights, own, peer, pairs[second])

    noise = noise_var[None, :]
    even = lax.axis_index("core") == 0
    lent = lax.all_gather(peer, "core")
    first_total = own + jnp.where(even, lent[1], lent[0])
    image = noise * targets + first_total
    block = gathered((targets - SIGMA * image).astype(BF16), ("x", "y_hi"))
    images = lax.all_gather(jnp.concatenate([targets, image], axis=0), "core")
    far, *pairs = halo(block)
    early = call(early_sums, shape(2, 2 * RHS))(targets, image)
    own, peer = call(apply_first, (half, half))(kernel_own, block)
    for kind in "FAB":
        if kind == "F":
            peer = call(apply_far, half)(kernels[kind], peer, far)
        else:
            own, peer = call(apply_pair, (half, half))(kernels[kind], own, peer, pairs["AB".index(kind)])
    sums = call(late_sums, shape(4, 2 * RHS))(
        early, noise, images, targets, image, first_total, own, peer
    )
    lent = lax.all_gather(peer, "core")
    second = noise * image + (first_total - own - jnp.where(even, lent[1], lent[0])) * (1.0 / SIGMA)
    for axes in (("x", "y_hi", "y_lo"), ("z", "core")):
        sums = jnp.sum(gathered(sums, axes), axis=0)

    (rr, rq), (qq, _), (rs, qs) = ((sums[i, :RHS], sums[i, RHS:]) for i in range(3))
    step = rr / rq
    norm_next = jnp.maximum(rr - 2.0 * step * rq + step * step * qq, 0.0)
    grown = 1.0 + norm_next / rr
    curvature = grown * grown * rq - step * grown * (qq + rs) + step * step * qs
    step_next = norm_next / curvature
    along = (step + step_next * grown)[:, None]
    across = (step_next * step)[:, None]
    solution = along * targets - across * image
    residual = targets - along * image + across * second
    return solution, residual


def solution(mesh):
    fine = Mesh(mesh.devices.reshape(SIZES), AXES)
    placed = (P(None, AXES), P(), P(AXES), P(None, AXES))
    return jax.shard_map(
        body, mesh=fine, in_specs=placed, out_specs=(P(None, AXES), P(None, AXES)), check_vma=False
    )
```

```python
import functools
import math

import jax
import jax.numpy as jnp
from jax import lax
from jax.experimental import pallas as pl
from jax.experimental.pallas import tpu as pltpu
from jax.sharding import Mesh, PartitionSpec as P

F32, BF16 = jnp.float32, jnp.bfloat16
AXES = ("y_lo", "z", "core", "x", "y_hi")
SIZES = (4, 8, 2, 4, 2)
BLK = ("y_lo", "z", "core")
N_BLK = 64
SWAP = ((0, 1), (1, 0))

LN2 = math.log(2.0)
UNIT = math.sqrt(5.0) / LN2
GRID = 2.0 / 1.5
SPAN = UNIT / GRID
SHIFT = 1.5 / LN2
OFFSET = 0.75 / LN2**2
LEVEL = math.log2(LN2**2 / 3.0) + SHIFT
LEVELS = tuple(LEVEL + math.log2(taper) for taper in (1.0, 0.75, 0.5, 0.25))
TINY = 1e-20

FEAT = 32
RHS = 64
WIDTH = 256
DEPTH = 80
SHARDS = 4
ROWS = 2 * WIDTH
SIGMA = 0.5
NT = (((1,), (1,)), ((), ()))


def square_rows(coords, first, second):
    squares = jnp.sum(coords * coords, axis=0, keepdims=True) * SPAN**2
    one = squares.astype(BF16).astype(F32)
    two = (squares - one).astype(BF16).astype(F32)
    three = squares - one - two
    row = lax.broadcasted_iota(jnp.int32, (16, coords.shape[1]), 0)
    out = jnp.where((row >= second) & (row < second + 3), 1.0, 0.0)
    for at, piece in enumerate((one, two, three)):
        out = jnp.where(row == first + at, piece, out)
    return out


def build_shard(weights, levels, shard, cols_ref, dist_ref, kernel_ref):
    coords = shard[:FEAT]
    cols_ref[:FEAT] = coords
    cols_ref[FEAT : 2 * FEAT] = coords
    cols_ref[2 * FEAT :] = square_rows(coords.astype(F32), 0, 3).astype(BF16)
    dist_ref[...] = jnp.dot(weights, cols_ref[...], preferred_element_type=F32)
    step = 64
    for half, level in enumerate(levels):
        for at in range(half * ROWS, (half + 1) * ROWS, step):
            part = jnp.maximum(dist_ref[at : at + step], TINY)
            moved = part * lax.rsqrt(part) + SHIFT
            entry = (moved * moved + OFFSET) * jnp.exp2(level - moved)
            kernel_ref[at : at + step] = entry.astype(BF16)
    return lax.dot_general(shard[FEAT:], kernel_ref[...], NT, preferred_element_type=F32)


def build_block(weights, levels, block_ref, cols_ref, dist_ref, kernel_ref):
    total = None
    for i in range(SHARDS):
        part = build_shard(weights, levels, block_ref[i], cols_ref.at[i % 2], dist_ref.at[i % 2], kernel_ref.at[i])
        total = part if total is None else total + part
    return total


def build_first(scale_ref, both_ref, block_ref, weights_ref, own_ref, peer_ref, kernel_ref, cols_ref, dist_ref):
    core = lax.axis_index("core")
    row = lax.broadcasted_iota(jnp.int32, (FEAT, FEAT), 0)
    column = lax.broadcasted_iota(jnp.int32, (FEAT, FEAT), 1)
    scale = GRID / jnp.sum(jnp.where(row == column, scale_ref[...], 0.0), axis=1, keepdims=True)
    for at, ref in enumerate(both_ref.at[which, peer] for which in (core, 1 - core) for peer in range(2)):
        rows = slice(at * WIDTH, (at + 1) * WIDTH)
        coords = ref[:FEAT] * scale
        scaled = coords * (-2.0 * SPAN**2)
        high = scaled.astype(BF16).astype(F32)
        stacked = jnp.concatenate([high, scaled - high, square_rows(coords, 3, 0)], axis=0)
        weights_ref[rows] = jnp.transpose(stacked).astype(BF16)
    total = build_block(weights_ref[...], LEVELS[:2], block_ref, cols_ref, dist_ref, kernel_ref)
    own_ref[...] = total[:, :ROWS]
    peer_ref[...] = total[:, ROWS:]


def build_far(weights_ref, before_ref, block_ref, peer_ref, kernel_ref, cols_ref, dist_ref):
    peer_ref[...] = before_ref[...] + build_block(
        weights_ref[ROWS:], LEVELS[3:], block_ref, cols_ref, dist_ref, kernel_ref
    )


def build_pair(
    second, weights_ref, own_before, peer_before, block_ref, own_ref, peer_ref, kernel_ref, cols_ref, dist_ref
):
    near = (lax.axis_index("z") + lax.axis_index("core") + second) % 2 == 0
    levels = LEVELS[2], jnp.where(near, LEVELS[1], LEVELS[3])
    total = build_block(weights_ref[...], levels, block_ref, cols_ref, dist_ref, kernel_ref)
    own_ref[...] = own_before[...] + total[:, :ROWS]
    peer_ref[...] = peer_before[...] + total[:, ROWS:]


def apply_block(kernel_ref, block_ref):
    total = None
    for i in range(SHARDS):
        part = lax.dot_general(block_ref[i], kernel_ref[i], NT, preferred_element_type=F32)
        total = part if total is None else total + part
    return total


def apply_first(kernel_ref, block_ref, own_ref, peer_ref):
    total = apply_block(kernel_ref, block_ref)
    own_ref[...] = total[:, :ROWS]
    peer_ref[...] = total[:, ROWS:]


def apply_far(kernel_ref, before_ref, block_ref, peer_ref):
    peer_ref[...] = before_ref[...] + apply_block(kernel_ref, block_ref)


def apply_pair(kernel_ref, own_before, peer_before, block_ref, own_ref, peer_ref):
    total = apply_block(kernel_ref, block_ref)
    own_ref[...] = own_before[...] + total[:, :ROWS]
    peer_ref[...] = peer_before[...] + total[:, ROWS:]


def row_sum(product):
    ones = jnp.ones((8, WIDTH), F32)
    total = lax.dot_general(ones, product, NT, precision=lax.Precision.HIGHEST, preferred_element_type=F32)
    return total[:1]


def early_sums(first_ref, image_ref, sums_ref):
    first, image = first_ref[...], image_ref[...]
    sums_ref[0:1, :RHS] = row_sum(first * first)
    sums_ref[0:1, RHS:] = row_sum(first * image)
    sums_ref[1:2, :RHS] = row_sum(image * image)
    sums_ref[1:2, RHS:] = jnp.zeros((1, RHS), F32)


def late_sums(
    early_ref, noise_ref, first_ref, image_ref, first_total_ref, firsts_ref, images_ref, own_ref, peer_ref, sums_ref
):
    core = lax.axis_index("core")
    image = image_ref[...]
    known = noise_ref[...] * image + first_total_ref[...] * (1.0 / SIGMA)
    rows = [first_ref[...] * known, image * known]
    for which, part_ref in ((core, own_ref), (1 - core, peer_ref)):
        for peer in range(2):
            sent = part_ref[:, peer * WIDTH : (peer + 1) * WIDTH] * (1.0 / SIGMA)
            rows[0] -= firsts_ref[which, peer, FEAT:] * sent
            rows[1] -= images_ref[which, peer] * sent
    sums_ref[0:2] = early_ref[...]
    sums_ref[2:3, :RHS] = row_sum(rows[0])
    sums_ref[2:3, RHS:] = row_sum(rows[1])
    sums_ref[3:4] = jnp.zeros((1, 2 * RHS), F32)


VMEM_LIMIT = pltpu.CompilerParams(vmem_limit_bytes=20 * 1024 * 1024)


def scratch(rows=2 * ROWS):
    return [pltpu.VMEM((2, DEPTH, WIDTH), BF16), pltpu.VMEM((2, rows, WIDTH), F32)]


def shape(*dims, dtype=F32):
    return jax.ShapeDtypeStruct(dims, dtype)


def gathered(value, axes):
    count = math.prod(SIZES[AXES.index(axis)] for axis in axes)
    return lax.all_to_all(jnp.broadcast_to(value[None], (count,) + value.shape), axes, 0, 0)


def halo(block):
    first = [(i, i + 2 if i // 2 % 2 == 0 else i - 2) for i in range(N_BLK)]
    second = [(i, (i - 2 if i // 2 % 2 == 0 else i + 2) % N_BLK) for i in range(N_BLK)]
    fourth = [(i, (i - 4 if i % 2 == 0 else i + 4) % N_BLK) for i in range(N_BLK)]
    return tuple(lax.ppermute(block, BLK, route) for route in (fourth, first, second))


def kernel_shape(rows=2 * ROWS):
    return shape(SHARDS, rows, WIDTH, dtype=BF16)


def call(body, out_shape, scratch_shapes=()):
    return pl.pallas_call(body, out_shape=out_shape, scratch_shapes=scratch_shapes, compiler_params=VMEM_LIMIT)


def summed(own, peer):
    lent = lax.all_gather(peer, "core")
    total = own + jnp.where(lax.axis_index("core") == 0, lent[1], lent[0])
    return total[:, :WIDTH] + lax.ppermute(total[:, WIDTH:], "y_hi", SWAP)


def body(points, lengthscale, noise_var, targets):
    scale = GRID / jnp.pad(lengthscale, (0, RHS), constant_values=GRID)
    known = lax.optimization_barrier(jnp.concatenate([points, targets], axis=0))
    exact = known * scale[:, None]
    across = lax.ppermute(known, "y_hi", SWAP)
    block = gathered(exact.astype(BF16), ("x",))
    both = lax.all_gather(jnp.stack([known, across]), "core")
    far, *pairs = halo(block)

    half = shape(RHS, ROWS)
    weights, own, peer, kernel_own = call(
        build_first,
        (shape(2 * ROWS, DEPTH, dtype=BF16), half, half, kernel_shape()),
        scratch_shapes=scratch(),
    )(lengthscale[None], both, block)
    kernels = {}
    for kind in "ABF":
        if kind == "F":
            peer, kernels[kind] = call(build_far, (half, kernel_shape(ROWS)), scratch_shapes=scratch(ROWS))(
                weights, peer, far
            )
        else:
            second = "AB".index(kind)
            own, peer, kernels[kind] = call(
                functools.partial(build_pair, second), (half, half, kernel_shape()), scratch_shapes=scratch()
            )(weights, own, peer, pairs[second])

    noise = noise_var[None, :]
    first_total = summed(own, peer)
    image = noise * targets + first_total
    block = gathered((targets - SIGMA * image).astype(BF16), ("x",))
    block, later = lax.optimization_barrier((block, image))
    across = lax.ppermute(later, "y_hi", SWAP)
    images = lax.all_gather(jnp.stack([image, across]), "core")
    far, *pairs = halo(block)
    early = call(early_sums, shape(2, 2 * RHS))(targets, image)
    own, peer = call(apply_first, (half, half))(kernel_own, block)
    for kind in "FBA":
        if kind == "F":
            peer = call(apply_far, half)(kernels[kind], peer, far)
        else:
            own, peer = call(apply_pair, (half, half))(kernels[kind], own, peer, pairs["AB".index(kind)])
    sums = call(late_sums, shape(4, 2 * RHS))(
        early, noise, targets, image, first_total, both, images, own, peer
    )
    second = noise * image + (first_total - summed(own, peer)) * (1.0 / SIGMA)
    for axes in (("x", "y_hi", "y_lo"), ("z", "core")):
        sums = jnp.sum(gathered(sums, axes), axis=0)

    (rr, rq), (qq, _), (rs, qs) = ((sums[i, :RHS], sums[i, RHS:]) for i in range(3))
    step = rr / rq
    norm_next = jnp.maximum(rr - 2.0 * step * rq + step * step * qq, 0.0)
    grown = 1.0 + norm_next / rr
    curvature = grown * grown * rq - step * grown * (qq + rs) + step * step * qs
    step_next = norm_next / curvature
    along = (step + step_next * grown)[:, None]
    across = (step_next * step)[:, None]
    solution = along * targets - across * image
    residual = targets - along * image + across * second
    return solution, residual


def solution(mesh):
    fine = Mesh(mesh.devices.reshape(SIZES), AXES)
    placed = (P(None, AXES), P(), P(AXES), P(None, AXES))
    return jax.shard_map(
        body, mesh=fine, in_specs=placed, out_specs=(P(None, AXES), P(None, AXES)), check_vma=False
    )
```

```python
import functools
import math

import jax
import jax.numpy as jnp
from jax import lax
from jax.experimental import pallas as pl
from jax.experimental.pallas import tpu as pltpu
from jax.sharding import Mesh, PartitionSpec as P

F32, BF16 = jnp.float32, jnp.bfloat16
AXES = ("y_lo", "z", "core", "x", "y_hi")
SIZES = (4, 8, 2, 4, 2)
BLK = ("y_lo", "z", "core")
N_BLK = 64
SWAP = ((0, 1), (1, 0))

LN2 = math.log(2.0)
UNIT = math.sqrt(5.0) / LN2
GRID = 2.0 / 1.5
SPAN = UNIT / GRID
SHIFT = 1.5 / LN2
OFFSET = 0.75 / LN2**2
LEVEL = math.log2(LN2**2 / 3.0) + SHIFT
LEVELS = tuple(LEVEL + math.log2(taper) for taper in (1.0, 0.75, 0.5, 0.25))
TINY = 1e-20

FEAT = 32
RHS = 64
WIDTH = 256
DEPTH = 80
SHARDS = 4
ROWS = 2 * WIDTH
SIGMA = 0.5
NT = (((1,), (1,)), ((), ()))


def square_rows(coords, first, second):
    squares = jnp.sum(coords * coords, axis=0, keepdims=True) * SPAN**2
    one = squares.astype(BF16).astype(F32)
    two = (squares - one).astype(BF16).astype(F32)
    three = squares - one - two
    row = lax.broadcasted_iota(jnp.int32, (16, coords.shape[1]), 0)
    out = jnp.where((row >= second) & (row < second + 3), 1.0, 0.0)
    for at, piece in enumerate((one, two, three)):
        out = jnp.where(row == first + at, piece, out)
    return out


def build_shard(weights, levels, shard, cols_ref, dist_ref, kernel_ref):
    coords = shard[:FEAT]
    cols_ref[:FEAT] = coords
    cols_ref[FEAT : 2 * FEAT] = coords
    cols_ref[2 * FEAT :] = square_rows(coords.astype(F32), 0, 3).astype(BF16)
    dist_ref[...] = jnp.dot(weights, cols_ref[...], preferred_element_type=F32)
    step = 64
    for half, level in enumerate(levels):
        for at in range(half * ROWS, (half + 1) * ROWS, step):
            part = jnp.maximum(dist_ref[at : at + step], TINY)
            moved = part * lax.rsqrt(part) + SHIFT
            entry = (moved * moved + OFFSET) * jnp.exp2(level - moved)
            kernel_ref[at : at + step] = entry.astype(BF16)
    return lax.dot_general(shard[FEAT:], kernel_ref[...], NT, preferred_element_type=F32)


def build_block(weights, levels, block_ref, cols_ref, dist_ref, kernel_ref):
    total = None
    for i in range(SHARDS):
        part = build_shard(weights, levels, block_ref[i], cols_ref.at[i % 2], dist_ref.at[i % 2], kernel_ref.at[i])
        total = part if total is None else total + part
    return total


def build_first(both_ref, block_ref, weights_ref, own_ref, peer_ref, kernel_ref, cols_ref, dist_ref):
    core = lax.axis_index("core")
    for at, ref in enumerate(both_ref.at[which, peer] for which in (core, 1 - core) for peer in range(2)):
        rows = slice(at * WIDTH, (at + 1) * WIDTH)
        coords = ref[:FEAT]
        scaled = coords * (-2.0 * SPAN**2)
        high = scaled.astype(BF16).astype(F32)
        stacked = jnp.concatenate([high, scaled - high, square_rows(coords, 3, 0)], axis=0)
        weights_ref[rows] = jnp.transpose(stacked).astype(BF16)
    total = build_block(weights_ref[...], LEVELS[:2], block_ref, cols_ref, dist_ref, kernel_ref)
    own_ref[...] = total[:, :ROWS]
    peer_ref[...] = total[:, ROWS:]


def build_far(weights_ref, before_ref, block_ref, peer_ref, kernel_ref, cols_ref, dist_ref):
    peer_ref[...] = before_ref[...] + build_block(
        weights_ref[ROWS:], LEVELS[3:], block_ref, cols_ref, dist_ref, kernel_ref
    )


def build_pair(
    second, weights_ref, own_before, peer_before, block_ref, own_ref, peer_ref, kernel_ref, cols_ref, dist_ref
):
    near = (lax.axis_index("z") + lax.axis_index("core") + second) % 2 == 0
    levels = LEVELS[2], jnp.where(near, LEVELS[1], LEVELS[3])
    total = build_block(weights_ref[...], levels, block_ref, cols_ref, dist_ref, kernel_ref)
    own_ref[...] = own_before[...] + total[:, :ROWS]
    peer_ref[...] = peer_before[...] + total[:, ROWS:]


def apply_block(kernel_ref, block_ref):
    total = None
    for i in range(SHARDS):
        part = lax.dot_general(block_ref[i], kernel_ref[i], NT, preferred_element_type=F32)
        total = part if total is None else total + part
    return total


def apply_first(kernel_ref, block_ref, own_ref, peer_ref):
    total = apply_block(kernel_ref, block_ref)
    own_ref[...] = total[:, :ROWS]
    peer_ref[...] = total[:, ROWS:]


def apply_far(kernel_ref, before_ref, block_ref, peer_ref):
    peer_ref[...] = before_ref[...] + apply_block(kernel_ref, block_ref)


def apply_pair(kernel_ref, own_before, peer_before, block_ref, own_ref, peer_ref):
    total = apply_block(kernel_ref, block_ref)
    own_ref[...] = own_before[...] + total[:, :ROWS]
    peer_ref[...] = peer_before[...] + total[:, ROWS:]


def row_sum(product):
    ones = jnp.ones((8, WIDTH), F32)
    total = lax.dot_general(ones, product, NT, precision=lax.Precision.HIGHEST, preferred_element_type=F32)
    return total[:1]


def early_sums(first_ref, image_ref, sums_ref):
    first, image = first_ref[...], image_ref[...]
    sums_ref[0:1, :RHS] = row_sum(first * first)
    sums_ref[0:1, RHS:] = row_sum(first * image)
    sums_ref[1:2, :RHS] = row_sum(image * image)
    sums_ref[1:2, RHS:] = jnp.zeros((1, RHS), F32)


def late_sums(
    early_ref, noise_ref, first_ref, image_ref, first_total_ref, firsts_ref, images_ref, own_ref, peer_ref, sums_ref
):
    core = lax.axis_index("core")
    image = image_ref[...]
    known = noise_ref[...] * image + first_total_ref[...] * (1.0 / SIGMA)
    rows = [first_ref[...] * known, image * known]
    for which, part_ref in ((core, own_ref), (1 - core, peer_ref)):
        for peer in range(2):
            sent = part_ref[:, peer * WIDTH : (peer + 1) * WIDTH] * (1.0 / SIGMA)
            rows[0] -= firsts_ref[which, peer, FEAT:] * sent
            rows[1] -= images_ref[which, peer] * sent
    sums_ref[0:2] = early_ref[...]
    sums_ref[2:3, :RHS] = row_sum(rows[0])
    sums_ref[2:3, RHS:] = row_sum(rows[1])
    sums_ref[3:4] = jnp.zeros((1, 2 * RHS), F32)


VMEM_LIMIT = pltpu.CompilerParams(vmem_limit_bytes=20 * 1024 * 1024)


def scratch(rows=2 * ROWS):
    return [pltpu.VMEM((2, DEPTH, WIDTH), BF16), pltpu.VMEM((2, rows, WIDTH), F32)]


def shape(*dims, dtype=F32):
    return jax.ShapeDtypeStruct(dims, dtype)


def gathered(value, axes):
    count = math.prod(SIZES[AXES.index(axis)] for axis in axes)
    return lax.all_to_all(jnp.broadcast_to(value[None], (count,) + value.shape), axes, 0, 0)


def halo(block):
    first = [(i, i + 2 if i // 2 % 2 == 0 else i - 2) for i in range(N_BLK)]
    second = [(i, (i - 2 if i // 2 % 2 == 0 else i + 2) % N_BLK) for i in range(N_BLK)]
    fourth = [(i, (i - 4 if i % 2 == 0 else i + 4) % N_BLK) for i in range(N_BLK)]
    return tuple(lax.ppermute(block, BLK, route) for route in (fourth, first, second))


def kernel_shape(rows=2 * ROWS):
    return shape(SHARDS, rows, WIDTH, dtype=BF16)


def call(body, out_shape, scratch_shapes=()):
    return pl.pallas_call(body, out_shape=out_shape, scratch_shapes=scratch_shapes, compiler_params=VMEM_LIMIT)


def summed(own, peer):
    lent = lax.all_gather(peer, "core")
    total = own + jnp.where(lax.axis_index("core") == 0, lent[1], lent[0])
    return total[:, :WIDTH] + lax.ppermute(total[:, WIDTH:], "y_hi", SWAP)


def body(points, lengthscale, noise_var, targets):
    scale = GRID / jnp.pad(lengthscale, (0, RHS), constant_values=GRID)
    known = lax.optimization_barrier(jnp.concatenate([points, targets], axis=0))
    exact = known * scale[:, None]
    across = lax.ppermute(known, "y_hi", SWAP)
    block = gathered(exact.astype(BF16), ("x",))
    both = lax.all_gather(jnp.stack([known, across]) * scale[:, None], "core")
    far, *pairs = halo(block)

    half = shape(RHS, ROWS)
    weights, own, peer, kernel_own = call(
        build_first,
        (shape(2 * ROWS, DEPTH, dtype=BF16), half, half, kernel_shape()),
        scratch_shapes=scratch(),
    )(both, block)
    kernels = {}
    for kind in "ABF":
        if kind == "F":
            peer, kernels[kind] = call(build_far, (half, kernel_shape(ROWS)), scratch_shapes=scratch(ROWS))(
                weights, peer, far
            )
        else:
            second = "AB".index(kind)
            own, peer, kernels[kind] = call(
                functools.partial(build_pair, second), (half, half, kernel_shape()), scratch_shapes=scratch()
            )(weights, own, peer, pairs[second])

    noise = noise_var[None, :]
    first_total = summed(own, peer)
    image = noise * targets + first_total
    block = gathered((targets - SIGMA * image).astype(BF16), ("x",))
    far, *pairs = halo(block)
    early = call(early_sums, shape(2, 2 * RHS))(targets, image)
    own, peer = call(apply_first, (half, half))(kernel_own, block)
    own, later = lax.optimization_barrier((own, image))
    across = lax.ppermute(later, "y_hi", SWAP)
    images = lax.all_gather(jnp.stack([image, across]), "core")
    for kind in "FBA":
        if kind == "F":
            peer = call(apply_far, half)(kernels[kind], peer, far)
        else:
            own, peer = call(apply_pair, (half, half))(kernels[kind], own, peer, pairs["AB".index(kind)])
    sums = call(late_sums, shape(4, 2 * RHS))(
        early, noise, targets, image, first_total, both, images, own, peer
    )
    second = noise * image + (first_total - summed(own, peer)) * (1.0 / SIGMA)
    for axes in (("x", "y_hi", "y_lo"), ("z", "core")):
        sums = jnp.sum(gathered(sums, axes), axis=0)

    (rr, rq), (qq, _), (rs, qs) = ((sums[i, :RHS], sums[i, RHS:]) for i in range(3))
    step = rr / rq
    norm_next = jnp.maximum(rr - 2.0 * step * rq + step * step * qq, 0.0)
    grown = 1.0 + norm_next / rr
    curvature = grown * grown * rq - step * grown * (qq + rs) + step * step * qs
    step_next = norm_next / curvature
    along = (step + step_next * grown)[:, None]
    across = (step_next * step)[:, None]
    solution = along * targets - across * image
    residual = targets - along * image + across * second
    return solution, residual


def solution(mesh):
    fine = Mesh(mesh.devices.reshape(SIZES), AXES)
    placed = (P(None, AXES), P(), P(AXES), P(None, AXES))
    return jax.shard_map(
        body, mesh=fine, in_specs=placed, out_specs=(P(None, AXES), P(None, AXES)), check_vma=False
    )
```

```python
import functools
import math

import jax
import jax.numpy as jnp
from jax import lax
from jax.experimental import pallas as pl
from jax.experimental.pallas import tpu as pltpu
from jax.sharding import Mesh, PartitionSpec as P

F32, BF16 = jnp.float32, jnp.bfloat16
AXES = ("y_lo", "z", "core", "x", "y_hi")
SIZES = (4, 8, 2, 4, 2)
BLK = ("y_lo", "z", "core")
N_BLK = 64
SWAP = ((0, 1), (1, 0))

LN2 = math.log(2.0)
UNIT = math.sqrt(5.0) / LN2
GRID = 2.0 / 1.5
SPAN = UNIT / GRID
SHIFT = 1.5 / LN2
OFFSET = 0.75 / LN2**2
LEVEL = math.log2(LN2**2 / 3.0) + SHIFT
LEVELS = tuple(LEVEL + math.log2(taper) for taper in (1.0, 0.75, 0.5, 0.25))
TINY = 1e-20

FEAT = 32
RHS = 64
WIDTH = 256
DEPTH = 80
SHARDS = 4
ROWS = 2 * WIDTH
SIGMA = 0.5
NT = (((1,), (1,)), ((), ()))


def square_rows(coords, first, second):
    squares = jnp.sum(coords * coords, axis=0, keepdims=True) * SPAN**2
    one = squares.astype(BF16).astype(F32)
    two = (squares - one).astype(BF16).astype(F32)
    three = squares - one - two
    row = lax.broadcasted_iota(jnp.int32, (16, coords.shape[1]), 0)
    out = jnp.where((row >= second) & (row < second + 3), 1.0, 0.0)
    for at, piece in enumerate((one, two, three)):
        out = jnp.where(row == first + at, piece, out)
    return out


def build_shard(weights, levels, shard, cols_ref, dist_ref, kernel_ref):
    coords = shard[:FEAT]
    cols_ref[:FEAT] = coords
    cols_ref[FEAT : 2 * FEAT] = coords
    cols_ref[2 * FEAT :] = square_rows(coords.astype(F32), 0, 3).astype(BF16)
    dist_ref[...] = jnp.dot(weights, cols_ref[...], preferred_element_type=F32)
    step = 64
    for half, level in enumerate(levels):
        for at in range(half * ROWS, (half + 1) * ROWS, step):
            part = jnp.maximum(dist_ref[at : at + step], TINY)
            moved = part * lax.rsqrt(part) + SHIFT
            entry = (moved * moved + OFFSET) * jnp.exp2(level - moved)
            kernel_ref[at : at + step] = entry.astype(BF16)
    return lax.dot_general(shard[FEAT:], kernel_ref[...], NT, preferred_element_type=F32)


def build_block(weights, levels, block_ref, cols_ref, dist_ref, kernel_ref):
    total = None
    for i in range(SHARDS):
        part = build_shard(weights, levels, block_ref[i], cols_ref.at[i % 2], dist_ref.at[i % 2], kernel_ref.at[i])
        total = part if total is None else total + part
    return total


def build_first(both_ref, block_ref, weights_ref, own_ref, peer_ref, kernel_ref, cols_ref, dist_ref):
    core = lax.axis_index("core")
    for at, ref in enumerate(both_ref.at[which, peer] for which in (core, 1 - core) for peer in range(2)):
        rows = slice(at * WIDTH, (at + 1) * WIDTH)
        coords = ref[:FEAT]
        scaled = coords * (-2.0 * SPAN**2)
        high = scaled.astype(BF16).astype(F32)
        stacked = jnp.concatenate([high, scaled - high, square_rows(coords, 3, 0)], axis=0)
        weights_ref[rows] = jnp.transpose(stacked).astype(BF16)
    total = build_block(weights_ref[...], LEVELS[:2], block_ref, cols_ref, dist_ref, kernel_ref)
    own_ref[...] = total[:, :ROWS]
    peer_ref[...] = total[:, ROWS:]


def build_far(weights_ref, before_ref, block_ref, peer_ref, kernel_ref, cols_ref, dist_ref):
    peer_ref[...] = before_ref[...] + build_block(
        weights_ref[ROWS:], LEVELS[3:], block_ref, cols_ref, dist_ref, kernel_ref
    )


def build_pair(
    second, weights_ref, own_before, peer_before, block_ref, own_ref, peer_ref, kernel_ref, cols_ref, dist_ref
):
    near = (lax.axis_index("z") + lax.axis_index("core") + second) % 2 == 0
    levels = LEVELS[2], jnp.where(near, LEVELS[1], LEVELS[3])
    total = build_block(weights_ref[...], levels, block_ref, cols_ref, dist_ref, kernel_ref)
    own_ref[...] = own_before[...] + total[:, :ROWS]
    peer_ref[...] = peer_before[...] + total[:, ROWS:]


def apply_block(kernel_ref, block_ref):
    total = None
    for i in range(SHARDS):
        part = lax.dot_general(block_ref[i], kernel_ref[i], NT, preferred_element_type=F32)
        total = part if total is None else total + part
    return total


def apply_first(kernel_ref, block_ref, own_ref, peer_ref):
    total = apply_block(kernel_ref, block_ref)
    own_ref[...] = total[:, :ROWS]
    peer_ref[...] = total[:, ROWS:]


def apply_far(kernel_ref, before_ref, block_ref, peer_ref):
    peer_ref[...] = before_ref[...] + apply_block(kernel_ref, block_ref)


def apply_pair(kernel_ref, own_before, peer_before, block_ref, own_ref, peer_ref):
    total = apply_block(kernel_ref, block_ref)
    own_ref[...] = own_before[...] + total[:, :ROWS]
    peer_ref[...] = peer_before[...] + total[:, ROWS:]


def row_sum(product):
    ones = jnp.ones((8, WIDTH), F32)
    total = lax.dot_general(ones, product, NT, precision=lax.Precision.HIGHEST, preferred_element_type=F32)
    return total[:1]


def early_sums(first_ref, image_ref, sums_ref):
    first, image = first_ref[...], image_ref[...]
    sums_ref[0:1, :RHS] = row_sum(first * first)
    sums_ref[0:1, RHS:] = row_sum(first * image)
    sums_ref[1:2, :RHS] = row_sum(image * image)
    sums_ref[1:2, RHS:] = jnp.zeros((1, RHS), F32)


def late_sums(
    early_ref, noise_ref, first_ref, image_ref, first_total_ref, firsts_ref, images_ref, own_ref, peer_ref, sums_ref
):
    core = lax.axis_index("core")
    image = image_ref[...]
    known = noise_ref[...] * image + first_total_ref[...] * (1.0 / SIGMA)
    rows = [first_ref[...] * known, image * known]
    for which, part_ref in ((core, own_ref), (1 - core, peer_ref)):
        for peer in range(2):
            sent = part_ref[:, peer * WIDTH : (peer + 1) * WIDTH] * (1.0 / SIGMA)
            rows[0] -= firsts_ref[which, peer, FEAT:] * sent
            rows[1] -= images_ref[which, peer] * sent
    sums_ref[0:2] = early_ref[...]
    sums_ref[2:3, :RHS] = row_sum(rows[0])
    sums_ref[2:3, RHS:] = row_sum(rows[1])
    sums_ref[3:4] = jnp.zeros((1, 2 * RHS), F32)


VMEM_LIMIT = pltpu.CompilerParams(vmem_limit_bytes=20 * 1024 * 1024)


def scratch(rows=2 * ROWS):
    return [pltpu.VMEM((2, DEPTH, WIDTH), BF16), pltpu.VMEM((2, rows, WIDTH), F32)]


def shape(*dims, dtype=F32):
    return jax.ShapeDtypeStruct(dims, dtype)


def gathered(value, axes):
    count = math.prod(SIZES[AXES.index(axis)] for axis in axes)
    return lax.all_to_all(jnp.broadcast_to(value[None], (count,) + value.shape), axes, 0, 0)


def halo(block):
    first = [(i, i + 2 if i // 2 % 2 == 0 else i - 2) for i in range(N_BLK)]
    second = [(i, (i - 2 if i // 2 % 2 == 0 else i + 2) % N_BLK) for i in range(N_BLK)]
    fourth = [(i, (i - 4 if i % 2 == 0 else i + 4) % N_BLK) for i in range(N_BLK)]
    return tuple(lax.ppermute(block, BLK, route) for route in (fourth, first, second))


def kernel_shape(rows=2 * ROWS):
    return shape(SHARDS, rows, WIDTH, dtype=BF16)


def call(body, out_shape, scratch_shapes=()):
    return pl.pallas_call(body, out_shape=out_shape, scratch_shapes=scratch_shapes, compiler_params=VMEM_LIMIT)


def summed(own, peer):
    lent = lax.all_gather(peer, "core")
    total = own + jnp.where(lax.axis_index("core") == 0, lent[1], lent[0])
    return total[:, :WIDTH] + lax.ppermute(total[:, WIDTH:], "y_hi", SWAP)


def body(points, lengthscale, noise_var, targets):
    scale = GRID / jnp.pad(lengthscale, (0, RHS), constant_values=GRID)
    known = lax.optimization_barrier(jnp.concatenate([points, targets], axis=0))
    exact = known * scale[:, None]
    across = lax.ppermute(known, "y_hi", SWAP)
    block = gathered(exact.astype(BF16), ("x",))
    both = lax.all_gather(jnp.stack([known, across]) * scale[:, None], "core")
    far, *pairs = halo(block)

    half = shape(RHS, ROWS)
    weights, own, peer, kernel_own = call(
        build_first,
        (shape(2 * ROWS, DEPTH, dtype=BF16), half, half, kernel_shape()),
        scratch_shapes=scratch(),
    )(both, block)
    kernels = {}
    for kind in "ABF":
        if kind == "F":
            peer, kernels[kind] = call(build_far, (half, kernel_shape(ROWS)), scratch_shapes=scratch(ROWS))(
                weights, peer, far
            )
        else:
            second = "AB".index(kind)
            own, peer, kernels[kind] = call(
                functools.partial(build_pair, second), (half, half, kernel_shape()), scratch_shapes=scratch()
            )(weights, own, peer, pairs[second])

    noise = noise_var[None, :]
    first_total = summed(own, peer)
    image = noise * targets + first_total
    block = gathered((targets - SIGMA * image).astype(BF16), ("x",))
    far, *pairs = halo(block)
    early = call(early_sums, shape(2, 2 * RHS))(targets, image)
    own, peer = call(apply_first, (half, half))(kernel_own, block)
    own, later = lax.optimization_barrier((own, image))
    across = lax.ppermute(later, "y_hi", SWAP)
    images = lax.all_gather(jnp.stack([image, across]), "core")
    for kind in "FBA":
        if kind == "F":
            peer = call(apply_far, half)(kernels[kind], peer, far)
        else:
            own, peer = call(apply_pair, (half, half))(kernels[kind], own, peer, pairs["AB".index(kind)])
    sums = call(late_sums, shape(4, 2 * RHS))(
        early, noise, targets, image, first_total, both, images, own, peer
    )
    second = noise * image + (first_total - summed(own, peer)) * (1.0 / SIGMA)
    for axes in (("z", "core"), ("x", "y_hi", "y_lo")):
        sums = jnp.sum(gathered(sums, axes), axis=0)

    (rr, rq), (qq, _), (rs, qs) = ((sums[i, :RHS], sums[i, RHS:]) for i in range(3))
    step = rr / rq
    norm_next = jnp.maximum(rr - 2.0 * step * rq + step * step * qq, 0.0)
    grown = 1.0 + norm_next / rr
    curvature = grown * grown * rq - step * grown * (qq + rs) + step * step * qs
    step_next = norm_next / curvature
    along = (step + step_next * grown)[:, None]
    across = (step_next * step)[:, None]
    solution = along * targets - across * image
    residual = targets - along * image + across * second
    return solution, residual


def solution(mesh):
    fine = Mesh(mesh.devices.reshape(SIZES), AXES)
    placed = (P(None, AXES), P(), P(AXES), P(None, AXES))
    return jax.shard_map(
        body, mesh=fine, in_specs=placed, out_specs=(P(None, AXES), P(None, AXES)), check_vma=False
    )
```

```python
import functools
import math

import jax
import jax.numpy as jnp
from jax import lax
from jax.experimental import pallas as pl
from jax.experimental.pallas import tpu as pltpu
from jax.sharding import Mesh, PartitionSpec as P

F32, BF16 = jnp.float32, jnp.bfloat16
AXES = ("y_lo", "z", "core", "x", "y_hi")
SIZES = (4, 8, 2, 4, 2)
BLK = ("y_lo", "z", "core")
N_BLK = 64
SWAP = ((0, 1), (1, 0))

LN2 = math.log(2.0)
UNIT = math.sqrt(5.0) / LN2
GRID = 2.0 / 1.5
SPAN = UNIT / GRID
SHIFT = 1.5 / LN2
OFFSET = 0.75 / LN2**2
LEVEL = math.log2(LN2**2 / 3.0) + SHIFT
LEVELS = tuple(LEVEL + math.log2(taper) for taper in (1.0, 0.75, 0.5, 0.25))
TINY = 1e-20

FEAT = 32
RHS = 64
WIDTH = 256
DEPTH = 80
SHARDS = 4
ROWS = 2 * WIDTH
SIGMA = 0.5
NT = (((1,), (1,)), ((), ()))


def prepare(known_ref, scale_ref, exact_ref, message_ref):
    row = lax.broadcasted_iota(jnp.int32, (FEAT, FEAT), 0)
    column = lax.broadcasted_iota(jnp.int32, (FEAT, FEAT), 1)
    scale = jnp.sum(jnp.where(row == column, scale_ref[...], 0.0), axis=1, keepdims=True)
    exact_ref[:FEAT] = known_ref[:FEAT] * (GRID / scale)
    exact_ref[FEAT:] = known_ref[FEAT:]
    message = exact_ref[...].astype(BF16)
    for i in range(SHARDS):
        message_ref[i] = message


def square_rows(coords, first, second):
    squares = jnp.sum(coords * coords, axis=0, keepdims=True) * SPAN**2
    one = squares.astype(BF16).astype(F32)
    two = (squares - one).astype(BF16).astype(F32)
    three = squares - one - two
    row = lax.broadcasted_iota(jnp.int32, (16, coords.shape[1]), 0)
    out = jnp.where((row >= second) & (row < second + 3), 1.0, 0.0)
    for at, piece in enumerate((one, two, three)):
        out = jnp.where(row == first + at, piece, out)
    return out


def build_shard(weights, levels, shard, cols_ref, dist_ref, kernel_ref):
    coords = shard[:FEAT]
    cols_ref[:FEAT] = coords
    cols_ref[FEAT : 2 * FEAT] = coords
    cols_ref[2 * FEAT :] = square_rows(coords.astype(F32), 0, 3).astype(BF16)
    dist_ref[...] = jnp.dot(weights, cols_ref[...], preferred_element_type=F32)
    step = 64
    for half, level in enumerate(levels):
        for at in range(half * ROWS, (half + 1) * ROWS, step):
            part = jnp.maximum(dist_ref[at : at + step], TINY)
            moved = part * lax.rsqrt(part) + SHIFT
            entry = (moved * moved + OFFSET) * jnp.exp2(level - moved)
            kernel_ref[at : at + step] = entry.astype(BF16)
    return lax.dot_general(shard[FEAT:], kernel_ref[...], NT, preferred_element_type=F32)


def build_block(weights, levels, block_ref, cols_ref, dist_ref, kernel_ref):
    total = None
    for i in range(SHARDS):
        part = build_shard(weights, levels, block_ref[i], cols_ref.at[i % 2], dist_ref.at[i % 2], kernel_ref.at[i])
        total = part if total is None else total + part
    return total


def build_first(both_ref, block_ref, weights_ref, own_ref, peer_ref, kernel_ref, cols_ref, dist_ref):
    core = lax.axis_index("core")
    for at, ref in enumerate(both_ref.at[which, peer] for which in (core, 1 - core) for peer in range(2)):
        rows = slice(at * WIDTH, (at + 1) * WIDTH)
        coords = ref[:FEAT]
        scaled = coords * (-2.0 * SPAN**2)
        high = scaled.astype(BF16).astype(F32)
        stacked = jnp.concatenate([high, scaled - high, square_rows(coords, 3, 0)], axis=0)
        weights_ref[rows] = jnp.transpose(stacked).astype(BF16)
    total = build_block(weights_ref[...], LEVELS[:2], block_ref, cols_ref, dist_ref, kernel_ref)
    own_ref[...] = total[:, :ROWS]
    peer_ref[...] = total[:, ROWS:]


def build_far(weights_ref, before_ref, block_ref, peer_ref, kernel_ref, cols_ref, dist_ref):
    peer_ref[...] = before_ref[...] + build_block(
        weights_ref[ROWS:], LEVELS[3:], block_ref, cols_ref, dist_ref, kernel_ref
    )


def build_pair(
    second, weights_ref, own_before, peer_before, block_ref, own_ref, peer_ref, kernel_ref, cols_ref, dist_ref
):
    near = (lax.axis_index("z") + lax.axis_index("core") + second) % 2 == 0
    levels = LEVELS[2], jnp.where(near, LEVELS[1], LEVELS[3])
    total = build_block(weights_ref[...], levels, block_ref, cols_ref, dist_ref, kernel_ref)
    own_ref[...] = own_before[...] + total[:, :ROWS]
    peer_ref[...] = peer_before[...] + total[:, ROWS:]


def apply_block(kernel_ref, block_ref):
    total = None
    for i in range(SHARDS):
        part = lax.dot_general(block_ref[i], kernel_ref[i], NT, preferred_element_type=F32)
        total = part if total is None else total + part
    return total


def apply_first(kernel_ref, block_ref, own_ref, peer_ref):
    total = apply_block(kernel_ref, block_ref)
    own_ref[...] = total[:, :ROWS]
    peer_ref[...] = total[:, ROWS:]


def apply_far(kernel_ref, before_ref, block_ref, peer_ref):
    peer_ref[...] = before_ref[...] + apply_block(kernel_ref, block_ref)


def apply_pair(kernel_ref, own_before, peer_before, block_ref, own_ref, peer_ref):
    total = apply_block(kernel_ref, block_ref)
    own_ref[...] = own_before[...] + total[:, :ROWS]
    peer_ref[...] = peer_before[...] + total[:, ROWS:]


def row_sum(product):
    ones = jnp.ones((8, WIDTH), F32)
    total = lax.dot_general(ones, product, NT, precision=lax.Precision.HIGHEST, preferred_element_type=F32)
    return total[:1]


def early_sums(first_ref, image_ref, sums_ref):
    first, image = first_ref[...], image_ref[...]
    sums_ref[0:1, :RHS] = row_sum(first * first)
    sums_ref[0:1, RHS:] = row_sum(first * image)
    sums_ref[1:2, :RHS] = row_sum(image * image)
    sums_ref[1:2, RHS:] = jnp.zeros((1, RHS), F32)


def late_sums(
    early_ref, noise_ref, first_ref, image_ref, first_total_ref, firsts_ref, images_ref, own_ref, peer_ref, sums_ref
):
    core = lax.axis_index("core")
    image = image_ref[...]
    known = noise_ref[...] * image + first_total_ref[...] * (1.0 / SIGMA)
    rows = [first_ref[...] * known, image * known]
    for which, part_ref in ((core, own_ref), (1 - core, peer_ref)):
        for peer in range(2):
            sent = part_ref[:, peer * WIDTH : (peer + 1) * WIDTH] * (1.0 / SIGMA)
            rows[0] -= firsts_ref[which, peer, FEAT:] * sent
            rows[1] -= images_ref[which, peer] * sent
    sums_ref[0:2] = early_ref[...]
    sums_ref[2:3, :RHS] = row_sum(rows[0])
    sums_ref[2:3, RHS:] = row_sum(rows[1])
    sums_ref[3:4] = jnp.zeros((1, 2 * RHS), F32)


VMEM_LIMIT = pltpu.CompilerParams(vmem_limit_bytes=20 * 1024 * 1024)


def scratch(rows=2 * ROWS):
    return [pltpu.VMEM((2, DEPTH, WIDTH), BF16), pltpu.VMEM((2, rows, WIDTH), F32)]


def shape(*dims, dtype=F32):
    return jax.ShapeDtypeStruct(dims, dtype)


def gathered(value, axes):
    count = math.prod(SIZES[AXES.index(axis)] for axis in axes)
    return lax.all_to_all(jnp.broadcast_to(value[None], (count,) + value.shape), axes, 0, 0)


def halo(block):
    first = [(i, i + 2 if i // 2 % 2 == 0 else i - 2) for i in range(N_BLK)]
    second = [(i, (i - 2 if i // 2 % 2 == 0 else i + 2) % N_BLK) for i in range(N_BLK)]
    fourth = [(i, (i - 4 if i % 2 == 0 else i + 4) % N_BLK) for i in range(N_BLK)]
    return tuple(lax.ppermute(block, BLK, route) for route in (fourth, first, second))


def kernel_shape(rows=2 * ROWS):
    return shape(SHARDS, rows, WIDTH, dtype=BF16)


def call(body, out_shape, scratch_shapes=()):
    return pl.pallas_call(body, out_shape=out_shape, scratch_shapes=scratch_shapes, compiler_params=VMEM_LIMIT)


def summed(own, peer):
    lent = lax.all_gather(peer, "core")
    total = own + jnp.where(lax.axis_index("core") == 0, lent[1], lent[0])
    return total[:, :WIDTH] + lax.ppermute(total[:, WIDTH:], "y_hi", SWAP)


def body(points, lengthscale, noise_var, targets):
    known = jnp.concatenate([points, targets], axis=0)
    exact, message = call(
        prepare, (shape(FEAT + RHS, WIDTH), shape(SHARDS, FEAT + RHS, WIDTH, dtype=BF16))
    )(known, lengthscale[None])
    across = lax.ppermute(exact, "y_hi", SWAP)
    block = lax.all_to_all(message, ("x",), 0, 0)
    both = lax.all_gather(jnp.stack([exact, across]), "core")
    far, *pairs = halo(block)

    half = shape(RHS, ROWS)
    weights, own, peer, kernel_own = call(
        build_first,
        (shape(2 * ROWS, DEPTH, dtype=BF16), half, half, kernel_shape()),
        scratch_shapes=scratch(),
    )(both, block)
    kernels = {}
    for kind in "ABF":
        if kind == "F":
            peer, kernels[kind] = call(build_far, (half, kernel_shape(ROWS)), scratch_shapes=scratch(ROWS))(
                weights, peer, far
            )
        else:
            second = "AB".index(kind)
            own, peer, kernels[kind] = call(
                functools.partial(build_pair, second), (half, half, kernel_shape()), scratch_shapes=scratch()
            )(weights, own, peer, pairs[second])

    noise = noise_var[None, :]
    first_total = summed(own, peer)
    image = noise * targets + first_total
    block = gathered((targets - SIGMA * image).astype(BF16), ("x",))
    far, *pairs = halo(block)
    early = call(early_sums, shape(2, 2 * RHS))(targets, image)
    own, peer = call(apply_first, (half, half))(kernel_own, block)
    own, later = lax.optimization_barrier((own, image))
    across = lax.ppermute(later, "y_hi", SWAP)
    images = lax.all_gather(jnp.stack([image, across]), "core")
    for kind in "FBA":
        if kind == "F":
            peer = call(apply_far, half)(kernels[kind], peer, far)
        else:
            own, peer = call(apply_pair, (half, half))(kernels[kind], own, peer, pairs["AB".index(kind)])
    sums = call(late_sums, shape(4, 2 * RHS))(
        early, noise, targets, image, first_total, both, images, own, peer
    )
    second = noise * image + (first_total - summed(own, peer)) * (1.0 / SIGMA)
    for axes in (("z", "core"), ("x", "y_hi", "y_lo")):
        sums = jnp.sum(gathered(sums, axes), axis=0)

    (rr, rq), (qq, _), (rs, qs) = ((sums[i, :RHS], sums[i, RHS:]) for i in range(3))
    step = rr / rq
    norm_next = jnp.maximum(rr - 2.0 * step * rq + step * step * qq, 0.0)
    grown = 1.0 + norm_next / rr
    curvature = grown * grown * rq - step * grown * (qq + rs) + step * step * qs
    step_next = norm_next / curvature
    along = (step + step_next * grown)[:, None]
    across = (step_next * step)[:, None]
    solution = along * targets - across * image
    residual = targets - along * image + across * second
    return solution, residual


def solution(mesh):
    fine = Mesh(mesh.devices.reshape(SIZES), AXES)
    placed = (P(None, AXES), P(), P(AXES), P(None, AXES))
    return jax.shard_map(
        body, mesh=fine, in_specs=placed, out_specs=(P(None, AXES), P(None, AXES)), check_vma=False
    )
```
